32 devices in a mesh: ta: 4 (over y, x), gz: 4 (over z), col: 2 (over core).
Axes of the slice: x: 2, y: 2, z: 4, core: 2. Of those that a mesh axis runs over, the one named last changes fastest.
Arguments:
- rhs_field: float32 [1, 96, 32, 16, 128], P(None, None, ('ta', 'col'), 'gz'), may hold values from -6 to 6
- link_weights: float32 [8, 32, 16, 128], P(None, ('ta', 'col'), 'gz'), may hold values from 0.4 to 1.6
- fine_blocks: float32 [9, 96, 96], replicated, may hold values from -1 to 5
- smoother: float32 [96, 96], replicated, may hold values from -1 to 1
- plane_next: int32 [4, 128], replicated, may hold values from 0 to 127, as said below
- aggregate: int32 [128], replicated, may hold values from 0 to 7, as said below
- restrict_map: float32 [96, 128], replicated, may hold values from -0.625 to 0.625
- prolong_map: float32 [128, 96], replicated, may hold values from -0.5 to 0.5
- coarse_blocks: float32 [9, 128, 128], replicated, may hold values from -1 to 5
- coarse_smoother: float32 [128, 128], replicated, may hold values from -1 to 1
- coarse_next: int32 [4, 8], replicated, may hold values from 0 to 7, as said below
Outputs:
- solution: float32 [1, 96, 32, 16, 128], P(None, None, ('ta', 'col'), 'gz')
- residual: float32 [1, 96, 32, 16, 128], P(None, None, ('ta', 'col'), 'gz')
The draws below stay inside these ranges and needn't reach their ends.
Inputs may be any that keep to these rules, and one draw needn't show every extreme that they name: `plane_next`: each row is an ordering of the plane sites; row 1 undoes row 0 and row 3 undoes row 2. `aggregate`: each coarse plane site is named by exactly 16 entries. `coarse_next`: each row is an ordering of the coarse plane sites; row 1 undoes row 0 and row 3 undoes row 2.
All inputs are finite; a program needn't handle non-finite values.
Results may differ from the reference program's by a relative error of at most 0.0003.
Values sent between devices are 32-bit elements; how exact they have to be, the bound alone decides.
A program may use at most 64 MiB of HBM per device.

```python
import math
import jax
import jax.numpy as jnp
from jax import lax

CF = 96
CC = 128
RHS = 1
PLANE = 128
AGG = 16
SWEEPS = 3
NT = 32
NZ = 16
CPLANE = 8


def noise_draw(key, shape):
    return jnp.clip(jax.random.normal(key, shape, jnp.float32), -5.0, 5.0)


def block_set(key, order):
    first, second = jax.random.split(key)
    center = 4.0 * jnp.eye(order, dtype=jnp.float32) + noise_draw(first, (order, order)) / jnp.sqrt(jnp.float32(order))
    hops = 0.25 * noise_draw(second, (8, order, order)) / jnp.sqrt(jnp.float32(order))
    return jnp.concatenate([center[None], hops], axis=0)


def smoother_draw(key, order):
    return 0.25 * jnp.eye(order, dtype=jnp.float32) + 0.06 * noise_draw(key, (order, order)) / jnp.sqrt(jnp.float32(order))


def neighbour_table(key, count):
    first, second = jax.random.split(key)
    forward_x = jax.random.permutation(first, count).astype(jnp.int32)
    forward_y = jax.random.permutation(second, count).astype(jnp.int32)
    back_x = jnp.argsort(forward_x).astype(jnp.int32)
    back_y = jnp.argsort(forward_y).astype(jnp.int32)
    return jnp.stack([forward_x, back_x, forward_y, back_y]).astype(jnp.int32)


def draw_fine_blocks(key, part):
    return block_set(jax.random.fold_in(key, 11), CF)


def draw_smoother(key, part):
    return smoother_draw(jax.random.fold_in(key, 12), CF)


def draw_coarse_blocks(key, part):
    return block_set(jax.random.fold_in(key, 13), CC)


def draw_coarse_smoother(key, part):
    return smoother_draw(jax.random.fold_in(key, 14), CC)


def draw_plane_next(key, part):
    return neighbour_table(jax.random.fold_in(key, 15), PLANE)


def draw_coarse_next(key, part):
    return neighbour_table(jax.random.fold_in(key, 16), CPLANE)


def draw_aggregate(key, part):
    order = jax.random.permutation(jax.random.fold_in(key, 17), PLANE).astype(jnp.int32)
    return (order // AGG).astype(jnp.int32)


def block_levels(stream_key, shape, cuts, least, high):
    def one(position, parts):
        draws = jax.random.uniform(jax.random.fold_in(jax.random.fold_in(stream_key, 6), position), (parts,), jnp.float32, least / len(cuts), high / len(cuts))
        return jnp.repeat(jnp.exp(draws), shape[position] // parts).reshape((-1,) + (1,) * (len(shape) - position - 1))

    factor_of = one(*cuts[0])
    for cut in cuts[1:]:
        factor_of = factor_of * one(*cut)
    return factor_of


def gaussian(rng, dims, spread, most, cuts=(), kind=jnp.bfloat16):
    factor_of = block_levels(rng, dims, cuts, -0.22, 0.18) if cuts else 1.0
    array = jax.random.normal(rng, dims, jnp.float32) * spread * factor_of
    return jnp.minimum(jnp.maximum(array, -most), most).astype(kind)


def setup_inputs(seed: int = 0) -> dict:
    splits = jax.random.split(jax.random.key(seed), 12)
    return {
        "rhs_field": gaussian(splits[0], (RHS, CF, NT, NZ, PLANE), 1.0, 6.0, ((2, 8), (3, 4)), jnp.float32),
        "link_weights": jnp.clip(jnp.exp(math.log(1.6) - 1.3862944 * jax.random.uniform(splits[1], (8, NT, NZ, PLANE), jnp.float32) ** block_levels(splits[1], (8, NT, NZ, PLANE), ((1, 8), (2, 4)), -0.2, 0.2)), 0.4, 1.6),
        "fine_blocks": draw_fine_blocks(jax.random.fold_in(splits[11], 71), 0),
        "smoother": draw_smoother(jax.random.fold_in(splits[11], 71), 0),
        "plane_next": draw_plane_next(jax.random.fold_in(splits[11], 71), 0),
        "aggregate": draw_aggregate(jax.random.fold_in(splits[11], 71), 0),
        "restrict_map": gaussian(splits[6], (CF, CC), CF ** -0.5, 0.625, (), jnp.float32),
        "prolong_map": gaussian(splits[7], (CC, CF), CC ** -0.5, 0.5, (), jnp.float32),
        "coarse_blocks": draw_coarse_blocks(jax.random.fold_in(splits[11], 71), 0),
        "coarse_smoother": draw_coarse_smoother(jax.random.fold_in(splits[11], 71), 0),
        "coarse_next": draw_coarse_next(jax.random.fold_in(splits[11], 71), 0),
    }


def block_fine(matrix, field):
    return jnp.einsum("ij,rjtzp->ritzp", matrix, field, precision=lax.Precision.HIGHEST)


def block_coarse(matrix, field):
    return jnp.einsum("ij,rtzqj->rtzqi", matrix, field, precision=lax.Precision.HIGHEST)


def reference(rhs_field, link_weights, fine_blocks, smoother, plane_next, aggregate, restrict_map, prolong_map, coarse_blocks, coarse_smoother, coarse_next):
    onehot = (aggregate[:, None] == jnp.arange(CPLANE, dtype=jnp.int32)[None, :]).astype(jnp.float32)

    def fine_apply(field):
        padded = jnp.pad(field, ((0, 0), (0, 0), (1, 1), (1, 1), (0, 0)), mode="wrap")
        output = block_fine(fine_blocks[0], field)
        for direction in range(8):
            if direction == 0:
                neighbour = padded[:, :, 2:, 1:-1]
            elif direction == 1:
                neighbour = padded[:, :, :-2, 1:-1]
            elif direction == 2:
                neighbour = padded[:, :, 1:-1, 2:]
            elif direction == 3:
                neighbour = padded[:, :, 1:-1, :-2]
            else:
                neighbour = jnp.take(field, plane_next[direction - 4], axis=4)
            output = output + link_weights[direction][None, None] * block_fine(fine_blocks[direction + 1], neighbour)
        return output

    def coarse_apply(field):
        padded = jnp.pad(field, ((0, 0), (1, 1), (1, 1), (0, 0), (0, 0)), mode="wrap")
        output = block_coarse(coarse_blocks[0], field)
        for direction in range(8):
            if direction == 0:
                neighbour = padded[:, 2:, 1:-1]
            elif direction == 1:
                neighbour = padded[:, :-2, 1:-1]
            elif direction == 2:
                neighbour = padded[:, 1:-1, 2:]
            elif direction == 3:
                neighbour = padded[:, 1:-1, :-2]
            else:
                neighbour = jnp.take(field, coarse_next[direction - 4], axis=3)
            output = output + block_coarse(coarse_blocks[direction + 1], neighbour)
        return output

    solution = block_fine(smoother, rhs_field)
    solution = solution + block_fine(smoother, rhs_field - fine_apply(solution))
    fine_residual = rhs_field - fine_apply(solution)
    summed = jnp.einsum("rctzp,pq->rctzq", fine_residual, onehot, precision=lax.Precision.HIGHEST)
    coarse_rhs = jnp.einsum("rctzq,ck->rtzqk", summed, restrict_map, precision=lax.Precision.HIGHEST)
    values = block_coarse(coarse_smoother, coarse_rhs)
    for sweep_index in range(SWEEPS):
        values = values + block_coarse(coarse_smoother, coarse_rhs - coarse_apply(values))
    lifted = jnp.einsum("rtzqk,kc->rctzq", values, prolong_map, precision=lax.Precision.HIGHEST)
    solution = solution + jnp.einsum("rctzq,pq->rctzp", lifted, onehot, precision=lax.Precision.HIGHEST)
    for sweep_index in range(2):
        solution = solution + block_fine(smoother, rhs_field - fine_apply(solution))
    residual = rhs_field - fine_apply(solution)
    return solution, residual
```

```python
import functools

import jax
import jax.numpy as jnp
from jax import lax
from jax.experimental import pallas as pl
from jax.experimental.pallas import tpu as pltpu
from jax.sharding import PartitionSpec as P

SWEEPS = 3
POST = 2
F32 = jnp.float32
BF16 = jnp.bfloat16
MESH = pl.DeviceIdType.MESH
NN = (((1,), (0,)), ((), ()))
NT = (((1,), (1,)), ((), ()))


def dot(a, b, dims=NN):
    return lax.dot_general(a, b, dims, preferred_element_type=F32)


def split(x):
    hi = x.astype(BF16)
    return hi, (x - hi.astype(F32)).astype(BF16)


def stacked(x, axis):
    return jnp.concatenate(split(x), axis=axis)


def left_product(pair, x, dims=NN):
    rows = pair.shape[0] // 2
    hi, lo = split(x)
    both = dot(pair, hi, dims)
    return both[:rows] + both[rows:] + dot(pair[:rows], lo, dims)


def right_product(x, pair):
    columns = pair.shape[1] // 2
    hi, lo = split(x)
    both = dot(hi, pair)
    return both[:, :columns] + both[:, columns:] + dot(lo, pair[:, :columns])


def kernel(
    sizes,
    rhs_ref, weight_ref, blocks_ref, smoother_ref, next_ref, aggregate_ref,
    restrict_ref, prolong_ref, coarse_ref, coarse_smoother_ref, coarse_next_ref,
    solution_ref, residual_ref,
    fields, values, solved, rest, coarse_rhs,
    near_pair, hop_pair, smooth_pair, shuffle, spread,
    restrict_pair, prolong_pair, coarse_near, coarse_hop, coarse_smooth, coarse_shuffle,
    send_sem, recv_sem,
):
    nt, nz, cf, plane, cplane, cc, ncol, nta, ngz = sizes
    sites = nt * nz
    ta, gz, col = lax.axis_index("ta"), lax.axis_index("gz"), lax.axis_index("col")
    ring = nta * ncol
    here = ta * ncol + col
    after, before = lax.rem(here + 1, ring), lax.rem(here + ring - 1, ring)
    t_after = {"ta": after // ncol, "col": lax.rem(after, ncol)}
    t_before = {"ta": before // ncol, "col": lax.rem(before, ncol)}
    z_after = {"gz": lax.rem(gz + 1, ngz)}
    z_before = {"gz": lax.rem(gz + ngz - 1, ngz)}

    barrier = pltpu.get_barrier_semaphore()
    for device in (t_after, t_before, z_after, z_before):
        pl.semaphore_signal(barrier, inc=1, device_id=device, device_id_type=MESH)
    pl.semaphore_wait(barrier, 4)

    def exchange(buffer, number):
        inner_t, inner_z = pl.ds(1, nt), pl.ds(1, nz)
        plans = (
            (buffer.at[inner_t, 1], buffer.at[inner_t, nz + 1], z_before),
            (buffer.at[inner_t, nz], buffer.at[inner_t, 0], z_after),
            (buffer.at[1, inner_z], buffer.at[nt + 1, inner_z], t_before),
            (buffer.at[nt, inner_z], buffer.at[0, inner_z], t_after),
        )
        copies = []
        for index, (source, target, device) in enumerate(plans):
            copy = pltpu.make_async_remote_copy(
                src_ref=source,
                dst_ref=target,
                send_sem=send_sem.at[number, index],
                recv_sem=recv_sem.at[number, index],
                device_id=device,
                device_id_type=MESH,
            )
            copy.start()
            copies.append(copy)
        return copies

    def arrive(copies):
        for copy in copies:
            copy.wait_recv()

    def smooth(buffer):
        for t in range(nt):
            wide = jnp.concatenate([rest[t, z] for z in range(nz)], axis=1)
            wide = left_product(smooth_pair[...], wide)
            for z in range(nz):
                buffer[t + 1, z + 1] = wide[:, z * plane:(z + 1) * plane]

    def near(buffer):
        for t in range(nt):
            own = [buffer[t + 1, z + 1] for z in range(nz)]
            rows = jnp.concatenate([stacked(v, 1) for v in own], axis=0)
            moved = dot(rows, shuffle[...])
            terms = [jnp.concatenate(own, axis=1)]
            for k in range(4):
                terms.append(jnp.concatenate([
                    moved[z * cf:(z + 1) * cf, k * plane:(k + 1) * plane]
                    * weight_ref[4 + k, t, z:z + 1]
                    for z in range(nz)
                ], axis=1))
            image = left_product(near_pair[...], jnp.concatenate(terms, axis=0))
            for z in range(nz):
                rest[t, z] -= image[:, z * plane:(z + 1) * plane]

    def hops(buffer):
        for t in range(nt):
            terms = []
            for k, (dt, dz) in enumerate(((2, 1), (0, 1), (1, 2), (1, 0))):
                terms.append(jnp.concatenate([
                    buffer[t + dt, z + dz] * weight_ref[k, t, z:z + 1]
                    for z in range(nz)
                ], axis=1))
            image = left_product(hop_pair[...], jnp.concatenate(terms, axis=0))
            for z in range(nz):
                rest[t, z] -= image[:, z * plane:(z + 1) * plane]

    def add(buffer):
        for t in range(nt):
            for z in range(nz):
                solved[t, z] += buffer[t + 1, z + 1]

    pending = []
    smooth_pair[...] = stacked(smoother_ref[...], 0)
    for t in range(nt):
        for z in range(nz):
            rest[t, z] = rhs_ref[pl.ds(t * nz + z, cf, stride=sites), :]
    first = fields.at[0]
    smooth(first)
    copies = exchange(first, 0)
    pending += copies

    near_pair[...] = stacked(
        jnp.concatenate([blocks_ref[k] for k in (0, 5, 6, 7, 8)], axis=1), 0
    )
    hop_pair[...] = stacked(jnp.concatenate([blocks_ref[k] for k in (1, 2, 3, 4)], axis=1), 0)
    line = lax.broadcasted_iota(jnp.int32, (plane, plane), 0)
    for k in range(4):
        chosen = jnp.where(line == next_ref[k:k + 1, :], 1.0, 0.0).astype(BF16)
        shuffle[:, k * plane:(k + 1) * plane] = jnp.concatenate([chosen, chosen], axis=0)
    for t in range(nt):
        for z in range(nz):
            solved[t, z] = first[t + 1, z + 1]
    near(first)

    crows = sites * cplane
    line = lax.broadcasted_iota(jnp.int32, (crows, plane), 0)
    for s in range(sites):
        chosen = jnp.where(line == aggregate_ref[...] + s * cplane, 1.0, 0.0).astype(BF16)
        spread[:, s * plane:(s + 1) * plane] = jnp.concatenate([chosen, chosen], axis=0)
    restrict_pair[...] = stacked(restrict_ref[...], 1)
    prolong_pair[...] = stacked(jnp.transpose(prolong_ref[...]), 0)
    coarse_near[...] = stacked(
        jnp.concatenate([jnp.transpose(coarse_ref[k]) for k in (0, 5, 6, 7, 8)], axis=0), 1
    )
    coarse_hop[...] = stacked(
        jnp.concatenate([jnp.transpose(coarse_ref[k]) for k in (1, 2, 3, 4)], axis=0), 1
    )
    coarse_smooth[...] = stacked(jnp.transpose(coarse_smoother_ref[...]), 1)
    column = lax.broadcasted_iota(jnp.int32, (cplane, crows), 1)
    within = lax.rem(column, cplane)
    tiling = jnp.where(lax.broadcasted_iota(jnp.int32, (cplane, crows), 0) == within, 1.0, 0.0)
    padded_next = jnp.concatenate(
        [coarse_next_ref[...].astype(F32), jnp.zeros((4, cplane), F32)], axis=0
    )
    targets = dot(padded_next.astype(BF16), tiling.astype(BF16))
    line = lax.broadcasted_iota(jnp.int32, (crows, crows), 0).astype(F32)
    column = lax.broadcasted_iota(jnp.int32, (crows, crows), 1)
    start = (column - lax.rem(column, cplane)).astype(F32)
    for k, opposite in enumerate((1, 0, 3, 2)):
        chosen = jnp.where(line == start + targets[opposite:opposite + 1, :], 1.0, 0.0)
        chosen = chosen.astype(BF16)
        coarse_shuffle[k * crows:(k + 1) * crows, :] = jnp.concatenate([chosen, chosen], axis=1)

    arrive(copies)
    hops(first)

    second = fields.at[1]
    smooth(second)
    copies = exchange(second, 1)
    pending += copies
    near(second)
    add(second)
    arrive(copies)
    hops(second)

    line = lax.broadcasted_iota(jnp.int32, (2 * cplane, plane), 0)
    gather = jnp.where(line == aggregate_ref[...], 1.0, 0.0).astype(BF16)
    gather = jnp.concatenate([gather, gather], axis=1)
    sums = [
        dot(gather, stacked(rest[t, z], 1), NT)[:cplane]
        for t in range(nt) for z in range(nz)
    ]
    coarse_rhs[...] = right_product(jnp.concatenate(sums, axis=0), restrict_pair[...])

    def put(buffer, flat):
        for t in range(nt):
            for z in range(nz):
                s = t * nz + z
                buffer[t + 1, z + 1] = flat[s * cplane:(s + 1) * cplane]

    def shifted(buffer, dt, dz):
        return jnp.concatenate(
            [buffer[t + dt, z + dz] for t in range(nt) for z in range(nz)], axis=0
        )

    current = right_product(coarse_rhs[...], coarse_smooth[...])
    for sweep in range(SWEEPS):
        buffer = values.at[sweep]
        put(buffer, current)
        copies = exchange(buffer, 2 + POST + sweep)
        pending += copies
        moved = dot(coarse_shuffle[...], stacked(current, 0))
        terms = [current] + [moved[k * crows:(k + 1) * crows] for k in range(4)]
        rest_coarse = coarse_rhs[...] - right_product(
            jnp.concatenate(terms, axis=1), coarse_near[...]
        )
        arrive(copies)
        terms = [shifted(buffer, dt, dz) for dt, dz in ((2, 1), (0, 1), (1, 2), (1, 0))]
        rest_coarse -= right_product(jnp.concatenate(terms, axis=1), coarse_hop[...])
        current += right_product(rest_coarse, coarse_smooth[...])
    buffer = values.at[SWEEPS]
    put(buffer, current)
    copies = exchange(buffer, 2 + POST + SWEEPS)
    pending += copies

    correction = fields.at[2 + POST]

    def prolong(flat, places):
        lifted = stacked(left_product(prolong_pair[...], flat, NT), 1)
        rows = flat.shape[0]
        wide = dot(lifted, spread[...])
        for s, (t, z) in enumerate(places):
            correction[t, z] = wide[:, s * plane:(s + 1) * plane]

    prolong(current, [(t + 1, z + 1) for t in range(nt) for z in range(nz)])
    near(correction)
    add(correction)
    arrive(copies)
    around = [(nt + 1, z + 1) for z in range(nz)] + [(0, z + 1) for z in range(nz)]
    around += [(t + 1, nz + 1) for t in range(nt)] + [(t + 1, 0) for t in range(nt)]
    for begin in range(0, len(around), sites):
        places = around[begin:begin + sites]
        flat = [buffer[t, z] for t, z in places]
        flat += [jnp.zeros((cplane, cc), F32)] * (sites - len(places))
        prolong(jnp.concatenate(flat, axis=0), places)
    hops(correction)

    for sweep in range(POST):
        buffer = fields.at[2 + sweep]
        smooth(buffer)
        copies = exchange(buffer, 2 + sweep)
        pending += copies
        near(buffer)
        add(buffer)
        if sweep == POST - 1:
            for t in range(nt):
                for z in range(nz):
                    solution_ref[pl.ds(t * nz + z, cf, stride=sites), :] = solved[t, z]
        arrive(copies)
        hops(buffer)
    for t in range(nt):
        for z in range(nz):
            residual_ref[pl.ds(t * nz + z, cf, stride=sites), :] = rest[t, z]
    for copy in pending:
        copy.wait_send()


def solution(mesh):
    def shards(
        rhs_field, link_weights, fine_blocks, smoother, plane_next, aggregate,
        restrict_map, prolong_map, coarse_blocks, coarse_smoother, coarse_next,
    ):
        _, cf, nt, nz, plane = rhs_field.shape
        cplane = coarse_next.shape[1]
        cc = coarse_smoother.shape[0]
        sites = nt * nz
        crows = sites * cplane
        sizes = (
            nt, nz, cf, plane, cplane, cc,
            mesh.shape["col"], mesh.shape["ta"], mesh.shape["gz"],
        )
        exchanges = 3 + POST + SWEEPS
        out = jax.ShapeDtypeStruct((cf * sites, plane), F32)
        vmem = pl.BlockSpec(memory_space=pltpu.VMEM)
        solved, residual = pl.pallas_call(
            functools.partial(kernel, sizes),
            out_shape=(out, out),
            in_specs=[vmem] * 11,
            out_specs=(vmem, vmem),
            scratch_shapes=[
                pltpu.VMEM((3 + POST, nt + 2, nz + 2, cf, plane), F32),
                pltpu.VMEM((1 + SWEEPS, nt + 2, nz + 2, cplane, cc), F32),
                pltpu.VMEM((nt, nz, cf, plane), F32),
                pltpu.VMEM((nt, nz, cf, plane), F32),
                pltpu.VMEM((crows, cc), F32),
                pltpu.VMEM((2 * cf, 5 * cf), BF16),
                pltpu.VMEM((2 * cf, 4 * cf), BF16),
                pltpu.VMEM((2 * cf, cf), BF16),
                pltpu.VMEM((2 * plane, 4 * plane), BF16),
                pltpu.VMEM((2 * crows, sites * plane), BF16),
                pltpu.VMEM((cf, 2 * cc), BF16),
                pltpu.VMEM((2 * cf, cc), BF16),
                pltpu.VMEM((5 * cc, 2 * cc), BF16),
                pltpu.VMEM((4 * cc, 2 * cc), BF16),
                pltpu.VMEM((cc, 2 * cc), BF16),
                pltpu.VMEM((4 * crows, 2 * crows), BF16),
                pltpu.SemaphoreType.DMA((exchanges, 4)),
                pltpu.SemaphoreType.DMA((exchanges, 4)),
            ],
            compiler_params=pltpu.CompilerParams(
                collective_id=0, has_side_effects=True, vmem_limit_bytes=48 * 1024 * 1024
            ),
        )(
            rhs_field.reshape(cf * sites, plane), link_weights, fine_blocks, smoother,
            plane_next, aggregate.reshape(1, plane), restrict_map, prolong_map,
            coarse_blocks, coarse_smoother, coarse_next,
        )
        return solved.reshape(rhs_field.shape), residual.reshape(rhs_field.shape)

    return jax.shard_map(
        shards,
        mesh=mesh,
        in_specs=(
            P(None, None, ("ta", "col"), "gz", None),
            P(None, ("ta", "col"), "gz", None),
            P(), P(), P(), P(), P(), P(), P(), P(), P(),
        ),
        out_specs=(
            P(None, None, ("ta", "col"), "gz", None),
            P(None, None, ("ta", "col"), "gz", None),
        ),
        check_vma=False,
    )
```

```python
import functools

import jax
import jax.numpy as jnp
from jax import lax
from jax.experimental import pallas as pl
from jax.experimental.pallas import tpu as pltpu
from jax.sharding import PartitionSpec as P

SWEEPS = 3
F32 = jnp.float32
BF16 = jnp.bfloat16
MESH = pl.DeviceIdType.MESH
NN = (((1,), (0,)), ((), ()))
NT = (((1,), (1,)), ((), ()))


def dot(a, b, dims=NN):
    return lax.dot_general(a, b, dims, preferred_element_type=F32)


def split(x):
    hi = x.astype(BF16)
    return hi, (x - hi.astype(F32)).astype(BF16)


def stacked(x, axis):
    return jnp.concatenate(split(x), axis=axis)


def left_product(pair, x, dims=NN):
    rows = pair.shape[0] // 2
    hi, lo = split(x)
    both = dot(pair, hi, dims)
    return both[:rows] + both[rows:] + dot(pair[:rows], lo, dims)


def right_product(x, pair):
    columns = pair.shape[1] // 2
    hi, lo = split(x)
    both = dot(hi, pair)
    return both[:, :columns] + both[:, columns:] + dot(lo, pair[:, :columns])


def kernel(
    sizes,
    rhs_hbm, weight_hbm, blocks_hbm, smoother_hbm, next_hbm, aggregate_hbm,
    restrict_hbm, prolong_hbm, coarse_hbm, coarse_smoother_hbm, coarse_next_hbm,
    solution_ref, residual_ref,
    rhs_ref, weight_ref, blocks_ref, smoother_ref, next_ref, aggregate_ref,
    restrict_ref, prolong_ref, coarse_ref, coarse_smoother_ref, coarse_next_ref,
    fields, values, solved, rest, weights, coarse_rhs,
    near_pair, hop_pair, t_pair, z_pair, z_up_pair, z_down_pair, smooth_pair, shuffle, spread,
    restrict_pair, prolong_pair, coarse_near, coarse_hop, coarse_smooth, coarse_shuffle,
    load_sem, send_sem, recv_sem,
):
    nt, nz, cf, plane, cplane, cc, ncol, nta, ngz = sizes
    sites = nt * nz
    ta, gz, col = lax.axis_index("ta"), lax.axis_index("gz"), lax.axis_index("col")
    ring = nta * ncol
    here = ta * ncol + col
    after, before = lax.rem(here + 1, ring), lax.rem(here + ring - 1, ring)
    t_after = {"ta": after // ncol, "col": lax.rem(after, ncol)}
    t_before = {"ta": before // ncol, "col": lax.rem(before, ncol)}
    z_after = {"gz": lax.rem(gz + 1, ngz)}
    z_before = {"gz": lax.rem(gz + ngz - 1, ngz)}
    diagonals = [{**t_side, **z_side} for t_side in (t_before, t_after) for z_side in (z_before, z_after)]

    loads = {}
    for index, (name, source, target) in enumerate((
        ("rhs", rhs_hbm, rhs_ref), ("smoother", smoother_hbm, smoother_ref),
        ("weights", weight_hbm, weight_ref), ("blocks", blocks_hbm, blocks_ref),
        ("next", next_hbm, next_ref), ("aggregate", aggregate_hbm, aggregate_ref),
        ("restrict", restrict_hbm, restrict_ref), ("prolong", prolong_hbm, prolong_ref),
        ("coarse", coarse_hbm, coarse_ref),
        ("coarse_smoother", coarse_smoother_hbm, coarse_smoother_ref),
        ("coarse_next", coarse_next_hbm, coarse_next_ref),
    )):
        loads[name] = pltpu.make_async_copy(source, target, load_sem.at[index])
        loads[name].start()

    barrier = pltpu.get_barrier_semaphore()
    for device in [t_after, t_before, z_after, z_before] + diagonals:
        pl.semaphore_signal(barrier, inc=1, device_id=device, device_id_type=MESH)
    pl.semaphore_wait(barrier, 8)

    pending = []

    def send(number, index, source, target, device):
        copy = pltpu.make_async_remote_copy(
            src_ref=source,
            dst_ref=target,
            send_sem=send_sem.at[number, index],
            recv_sem=recv_sem.at[number, index],
            device_id=device,
            device_id_type=MESH,
        )
        copy.start()
        pending.append(copy)
        return copy

    def send_z(buffer, number, pad, width=1):
        inner = pl.ds(pad, nt)
        low, high = pl.ds(pad, width), pl.ds(pad + nz - width, width)
        above, below = pl.ds(pad + nz, width), pl.ds(pad - width, width)
        return [
            send(number, 0, buffer.at[inner, low], buffer.at[inner, above], z_before),
            send(number, 1, buffer.at[inner, high], buffer.at[inner, below], z_after),
        ]

    def send_t(buffer, number, pad, width=1):
        inner = pl.ds(pad, nz)
        low, high = pl.ds(pad, width), pl.ds(pad + nt - width, width)
        above, below = pl.ds(pad + nt, width), pl.ds(pad - width, width)
        return [
            send(number, 2, buffer.at[low, inner], buffer.at[above, inner], t_before),
            send(number, 3, buffer.at[high, inner], buffer.at[below, inner], t_after),
        ]

    def arrive(copies):
        for copy in copies:
            copy.wait_recv()

    rows = [[(t, z) for z in range(nz)] for t in range(nt)]
    columns = [[(t, z) for t in range(nt)] for z in range(nz)]
    edges_first = [0, nz - 1] + list(range(1, nz - 1))
    around = [
        [(-1, z) for z in range(nz)], [(nt, z) for z in range(nz)],
        [(t, -1) for t in range(nt)], [(t, nz) for t in range(nt)],
    ]
    t_hops = ((0, 1, 0), (1, -1, 0))
    z_hops = ((2, 0, 1), (3, 0, -1))

    def lanes(x, s):
        return x[:, s * plane:(s + 1) * plane]

    def take(image, places):
        for s, (t, z) in enumerate(places):
            rest[t + 1, z + 1] -= lanes(image, s)

    def smooth(buffer, places):
        wide = jnp.concatenate([rest[t + 1, z + 1] for t, z in places], axis=1)
        wide = left_product(smooth_pair[...], wide)
        for s, (t, z) in enumerate(places):
            buffer[t + 2, z + 2] = lanes(wide, s)

    def near(buffer, places):
        own = [buffer[t + 2, z + 2] for t, z in places]
        moved = dot(jnp.concatenate([stacked(v, 1) for v in own], axis=0), shuffle[...])
        terms = [jnp.concatenate(own, axis=1)]
        for k in range(4):
            terms.append(jnp.concatenate([
                moved[s * cf:(s + 1) * cf, k * plane:(k + 1) * plane]
                * weights[t + 1, z + 1, 4 + k:5 + k]
                for s, (t, z) in enumerate(places)
            ], axis=1))
        take(left_product(near_pair[...], jnp.concatenate(terms, axis=0)), places)

    def hops(buffer, places, pair, shifts):
        terms = [
            jnp.concatenate([
                buffer[t + 2 + dt, z + 2 + dz] * weights[t + 1, z + 1, k:k + 1]
                for t, z in places
            ], axis=1)
            for k, dt, dz in shifts
        ]
        take(left_product(pair[...], jnp.concatenate(terms, axis=0)), places)

    def inner_z(buffer):
        hops(buffer, columns[0], z_up_pair, z_hops[:1])
        hops(buffer, columns[-1], z_down_pair, z_hops[1:])
        for places in columns[1:-1]:
            hops(buffer, places, z_pair, z_hops)

    def outer_z(buffer, z):
        if z == 0:
            hops(buffer, columns[0], z_down_pair, z_hops[1:])
        if z == nz - 1:
            hops(buffer, columns[-1], z_up_pair, z_hops[:1])

    def add(buffer):
        for t in range(nt):
            for z in range(nz):
                solved[t, z] += buffer[t + 2, z + 2]

    loads["rhs"].wait()
    loads["smoother"].wait()
    smooth_pair[...] = stacked(smoother_ref[...], 0)
    first = fields.at[0]
    for z in edges_first:
        for t in range(nt):
            rest[t + 1, z + 1] = rhs_ref[pl.ds(t * nz + z, cf, stride=sites), :]
        smooth(first, columns[z])
        if z == nz - 1:
            z_copies = send_z(first, 0, 2)
    t_copies = send_t(first, 0, 2)

    for name in ("weights", "blocks", "next"):
        loads[name].wait()
    for t in range(nt):
        for z in range(nz):
            weights[t + 1, z + 1] = weight_ref[pl.ds(t * nz + z, 8, stride=sites), :]
    weight_copies = send_z(weights, 4, 1) + send_t(weights, 4, 1)
    blocks = [blocks_ref[k] for k in range(9)]
    near_pair[...] = stacked(jnp.concatenate([blocks[k] for k in (0, 5, 6, 7, 8)], axis=1), 0)
    hop_pair[...] = stacked(jnp.concatenate(blocks[1:5], axis=1), 0)
    t_pair[...] = stacked(jnp.concatenate(blocks[1:3], axis=1), 0)
    z_pair[...] = stacked(jnp.concatenate(blocks[3:5], axis=1), 0)
    z_up_pair[...] = stacked(blocks[3], 0)
    z_down_pair[...] = stacked(blocks[4], 0)
    line = lax.broadcasted_iota(jnp.int32, (plane, plane), 0)
    for k in range(4):
        chosen = jnp.where(line == next_ref[k:k + 1, :], 1.0, 0.0).astype(BF16)
        shuffle[:, k * plane:(k + 1) * plane] = jnp.concatenate([chosen, chosen], axis=0)
    for t in range(nt):
        for z in range(nz):
            solved[t, z] = first[t + 2, z + 2]
    for places in rows:
        near(first, places)
    inner_z(first)

    for name in (
        "aggregate", "restrict", "prolong", "coarse", "coarse_smoother", "coarse_next"
    ):
        loads[name].wait()
    crows = sites * cplane
    line = lax.broadcasted_iota(jnp.int32, (crows, plane), 0)
    for s in range(sites):
        chosen = jnp.where(line == aggregate_ref[...] + s * cplane, 1.0, 0.0).astype(BF16)
        spread[:, s * plane:(s + 1) * plane] = jnp.concatenate([chosen, chosen], axis=0)
    restrict_pair[...] = stacked(restrict_ref[...], 1)
    prolong_pair[...] = stacked(prolong_ref[...], 0)
    coarse_near[...] = stacked(
        jnp.concatenate([jnp.transpose(coarse_ref[k]) for k in (0, 5, 6, 7, 8)], axis=0), 1
    )
    coarse_hop[...] = stacked(
        jnp.concatenate([jnp.transpose(coarse_ref[k]) for k in (1, 2, 3, 4)], axis=0), 1
    )
    coarse_smooth[...] = stacked(jnp.transpose(coarse_smoother_ref[...]), 1)
    column = lax.broadcasted_iota(jnp.int32, (cplane, crows), 1)
    within = lax.rem(column, cplane)
    tiling = jnp.where(lax.broadcasted_iota(jnp.int32, (cplane, crows), 0) == within, 1.0, 0.0)
    padded_next = jnp.concatenate(
        [coarse_next_ref[...].astype(F32), jnp.zeros((4, cplane), F32)], axis=0
    )
    targets = dot(padded_next.astype(BF16), tiling.astype(BF16))
    line = lax.broadcasted_iota(jnp.int32, (crows, crows), 0).astype(F32)
    column = lax.broadcasted_iota(jnp.int32, (crows, crows), 1)
    start = (column - lax.rem(column, cplane)).astype(F32)
    for k, opposite in enumerate((1, 0, 3, 2)):
        chosen = jnp.where(line == start + targets[opposite:opposite + 1, :], 1.0, 0.0)
        chosen = chosen.astype(BF16)
        coarse_shuffle[k * crows:(k + 1) * crows, :] = jnp.concatenate([chosen, chosen], axis=1)

    arrive(t_copies)
    for places in rows:
        hops(first, places, t_pair, t_hops)
    arrive(z_copies)

    second = fields.at[1]
    for z in edges_first:
        outer_z(first, z)
        smooth(second, columns[z])
        if z == nz - 1:
            z_copies = send_z(second, 1, 2)
    t_copies = send_t(second, 1, 2)
    for places in rows:
        near(second, places)
    inner_z(second)
    add(second)
    arrive(t_copies)
    for places in rows:
        hops(second, places, t_pair, t_hops)
    arrive(z_copies)
    outer_z(second, 0)
    outer_z(second, nz - 1)

    rest_copies = send_z(rest, 2, 1) + send_t(rest, 2, 1)

    line = lax.broadcasted_iota(jnp.int32, (2 * cplane, plane), 0)
    gather = jnp.where(line == aggregate_ref[...], 1.0, 0.0).astype(BF16)
    gather = jnp.concatenate([gather, gather], axis=1)
    sums = [
        dot(gather, stacked(rest[t + 1, z + 1], 1), NT)[:cplane]
        for t in range(nt) for z in range(nz)
    ]
    coarse_rhs[...] = right_product(jnp.concatenate(sums, axis=0), restrict_pair[...])

    def put(buffer, flat):
        for t in range(nt):
            for z in range(nz):
                s = t * nz + z
                buffer[t + 2, z + 2] = flat[s * cplane:(s + 1) * cplane]

    def shifted(buffer, dt, dz):
        return jnp.concatenate(
            [buffer[t + 2 + dt, z + 2 + dz] for t in range(nt) for z in range(nz)], axis=0
        )

    current = right_product(coarse_rhs[...], coarse_smooth[...])
    for sweep in range(SWEEPS):
        buffer = values.at[sweep]
        put(buffer, current)
        copies = send_z(buffer, 5 + sweep, 2) + send_t(buffer, 5 + sweep, 2)
        moved = dot(coarse_shuffle[...], stacked(current, 0))
        terms = [current] + [moved[k * crows:(k + 1) * crows] for k in range(4)]
        rest_coarse = coarse_rhs[...] - right_product(
            jnp.concatenate(terms, axis=1), coarse_near[...]
        )
        arrive(copies)
        terms = [shifted(buffer, dt, dz) for _, dt, dz in t_hops + z_hops]
        rest_coarse -= right_product(jnp.concatenate(terms, axis=1), coarse_hop[...])
        current += right_product(rest_coarse, coarse_smooth[...])
    buffer = values.at[SWEEPS]
    put(buffer, current)
    number = 5 + SWEEPS
    copies = send_z(buffer, number, 2, 2) + send_t(buffer, number, 2, 2)
    sides = [(t, z) for t in (0, 1) for z in (0, 1)]
    for index, (device, (t, z)) in enumerate(zip(diagonals, sides)):
        source = buffer.at[1 + nt if t else 2, 1 + nz if z else 2]
        target = buffer.at[1 if t else 2 + nt, 1 if z else 2 + nz]
        copies.append(send(number, 4 + index, source, target, device))

    correction = fields.at[2]

    def prolong(flat, places):
        lifted = stacked(left_product(prolong_pair[...], flat, NT), 1)
        wide = dot(lifted, spread[...])
        for s, (t, z) in enumerate(places):
            correction[t + 2, z + 2] = lanes(wide, s)

    prolong(current, [place for places in rows for place in places])
    for copy in rest_copies:
        copy.wait_send()
    pending[:] = [copy for copy in pending if not any(copy is done for done in rest_copies)]
    for places in rows:
        near(correction, places)
    inner_z(correction)
    add(correction)
    arrive(copies)
    halo = [place for places in around for place in places]
    halo += [(t, z) for t in (-2, nt + 1) for z in range(nz)]
    halo += [(t, z) for t in range(nt) for z in (-2, nz + 1)]
    halo += [(t, z) for t in (-1, nt) for z in (-1, nz)]
    for begin in range(0, len(halo), sites):
        places = halo[begin:begin + sites]
        flat = [buffer[t + 2, z + 2] for t, z in places]
        flat += [jnp.zeros((cplane, cc), F32)] * (sites - len(places))
        prolong(jnp.concatenate(flat, axis=0), places)
    for places in rows:
        hops(correction, places, t_pair, t_hops)
    outer_z(correction, 0)
    outer_z(correction, nz - 1)
    arrive(weight_copies)
    arrive(rest_copies)
    third = fields.at[3]
    for places in around:
        near(correction, places)
        hops(correction, places, hop_pair, t_hops + z_hops)
        smooth(third, places)
    for places in columns:
        smooth(third, places)

    last = fields.at[4]
    for z in edges_first:
        near(third, columns[z])
        hops(third, columns[z], hop_pair, t_hops + z_hops)
        smooth(last, columns[z])
        if z == nz - 1:
            z_copies = send_z(last, 3, 2)
    t_copies = send_t(last, 3, 2)
    for t in range(nt):
        for z in range(nz):
            solution_ref[pl.ds(t * nz + z, cf, stride=sites), :] = (
                solved[t, z] + third[t + 2, z + 2] + last[t + 2, z + 2]
            )
    for places in rows:
        near(last, places)
    inner_z(last)
    arrive(t_copies)
    for places in rows:
        hops(last, places, t_pair, t_hops)
    for places in columns[1:-1]:
        for t, z in places:
            residual_ref[pl.ds(t * nz + z, cf, stride=sites), :] = rest[t + 1, z + 1]
    arrive(z_copies)
    for places in (columns[0], columns[-1]):
        outer_z(last, places[0][1])
        for t, z in places:
            residual_ref[pl.ds(t * nz + z, cf, stride=sites), :] = rest[t + 1, z + 1]
    for copy in pending:
        copy.wait_send()


def solution(mesh):
    def shards(
        rhs_field, link_weights, fine_blocks, smoother, plane_next, aggregate,
        restrict_map, prolong_map, coarse_blocks, coarse_smoother, coarse_next,
    ):
        _, cf, nt, nz, plane = rhs_field.shape
        cplane = coarse_next.shape[1]
        cc = coarse_smoother.shape[0]
        sites = nt * nz
        crows = sites * cplane
        sizes = (
            nt, nz, cf, plane, cplane, cc,
            mesh.shape["col"], mesh.shape["ta"], mesh.shape["gz"],
        )
        out = jax.ShapeDtypeStruct((cf * sites, plane), F32)
        vmem = pl.BlockSpec(memory_space=pltpu.VMEM)
        hbm = pl.BlockSpec(memory_space=pltpu.HBM)
        operands = (
            rhs_field.reshape(cf * sites, plane), link_weights.reshape(-1, plane), fine_blocks,
            smoother, plane_next, aggregate.reshape(1, plane), restrict_map, prolong_map.T,
            coarse_blocks, coarse_smoother, coarse_next,
        )
        solved, residual = pl.pallas_call(
            functools.partial(kernel, sizes),
            out_shape=(out, out),
            in_specs=[hbm] * len(operands),
            out_specs=(vmem, vmem),
            scratch_shapes=[pltpu.VMEM(operand.shape, operand.dtype) for operand in operands] + [
                pltpu.VMEM((5, nt + 4, nz + 4, cf, plane), F32),
                pltpu.VMEM((1 + SWEEPS, nt + 4, nz + 4, cplane, cc), F32),
                pltpu.VMEM((nt, nz, cf, plane), F32),
                pltpu.VMEM((nt + 2, nz + 2, cf, plane), F32),
                pltpu.VMEM((nt + 2, nz + 2, 8, plane), F32),
                pltpu.VMEM((crows, cc), F32),
                pltpu.VMEM((2 * cf, 5 * cf), BF16),
                pltpu.VMEM((2 * cf, 4 * cf), BF16),
                pltpu.VMEM((2 * cf, 2 * cf), BF16),
                pltpu.VMEM((2 * cf, 2 * cf), BF16),
                pltpu.VMEM((2 * cf, cf), BF16),
                pltpu.VMEM((2 * cf, cf), BF16),
                pltpu.VMEM((2 * cf, cf), BF16),
                pltpu.VMEM((2 * plane, 4 * plane), BF16),
                pltpu.VMEM((2 * crows, sites * plane), BF16),
                pltpu.VMEM((cf, 2 * cc), BF16),
                pltpu.VMEM((2 * cf, cc), BF16),
                pltpu.VMEM((5 * cc, 2 * cc), BF16),
                pltpu.VMEM((4 * cc, 2 * cc), BF16),
                pltpu.VMEM((cc, 2 * cc), BF16),
                pltpu.VMEM((4 * crows, 2 * crows), BF16),
                pltpu.SemaphoreType.DMA((len(operands),)),
                pltpu.SemaphoreType.DMA((6 + SWEEPS, 8)),
                pltpu.SemaphoreType.DMA((6 + SWEEPS, 8)),
            ],
            compiler_params=pltpu.CompilerParams(
                collective_id=0, has_side_effects=True, vmem_limit_bytes=63 * 1024 * 1024
            ),
        )(*operands)
        return solved.reshape(rhs_field.shape), residual.reshape(rhs_field.shape)

    return jax.shard_map(
        shards,
        mesh=mesh,
        in_specs=(
            P(None, None, ("ta", "col"), "gz", None),
            P(None, ("ta", "col"), "gz", None),
            P(), P(), P(), P(), P(), P(), P(), P(), P(),
        ),
        out_specs=(
            P(None, None, ("ta", "col"), "gz", None),
            P(None, None, ("ta", "col"), "gz", None),
        ),
        check_vma=False,
    )
```

```python
import functools

import jax
import jax.numpy as jnp
from jax import lax
from jax.experimental import pallas as pl
from jax.experimental.pallas import tpu as pltpu
from jax.sharding import PartitionSpec as P

SWEEPS = 3
F32 = jnp.float32
BF16 = jnp.bfloat16
MESH = pl.DeviceIdType.MESH
NN = (((1,), (0,)), ((), ()))
NT = (((1,), (1,)), ((), ()))


def dot(a, b, dims=NN):
    return lax.dot_general(a, b, dims, preferred_element_type=F32)


def split(x):
    hi = x.astype(BF16)
    return hi, (x - hi.astype(F32)).astype(BF16)


def stacked(x, axis):
    return jnp.concatenate(split(x), axis=axis)


def left_product(pair, x, dims=NN):
    rows = pair.shape[0] // 2
    hi, lo = split(x)
    both = dot(pair, hi, dims)
    return both[:rows] + both[rows:] + dot(pair[:rows], lo, dims)


def right_product(x, pair):
    columns = pair.shape[1] // 2
    hi, lo = split(x)
    both = dot(hi, pair)
    return both[:, :columns] + both[:, columns:] + dot(lo, pair[:, :columns])


def kernel(
    sizes,
    rhs_hbm, weight_hbm, blocks_hbm, smoother_hbm, next_hbm, aggregate_hbm,
    restrict_hbm, prolong_hbm, coarse_hbm, coarse_smoother_hbm, coarse_next_hbm,
    solution_ref, residual_ref,
    rhs_ref, weight_ref, blocks_ref, smoother_ref, next_ref, aggregate_ref,
    restrict_ref, prolong_ref, coarse_ref, coarse_smoother_ref, coarse_next_ref,
    fields, values, weights, coarse_rhs,
    all_pairs, down_pairs, single_pairs, smooth_pair, shuffle, spread,
    restrict_pair, prolong_pair, coarse_near, coarse_hop, coarse_smooth, coarse_shuffle,
    load_sem, send_sem, recv_sem,
):
    nt, nz, cf, plane, cplane, cc, ncol, nta, ngz = sizes
    sites = nt * nz
    ta, gz, col = lax.axis_index("ta"), lax.axis_index("gz"), lax.axis_index("col")
    ring = nta * ncol
    here = ta * ncol + col
    after, before = lax.rem(here + 1, ring), lax.rem(here + ring - 1, ring)
    t_after = {"ta": after // ncol, "col": lax.rem(after, ncol)}
    t_before = {"ta": before // ncol, "col": lax.rem(before, ncol)}
    z_after = {"gz": lax.rem(gz + 1, ngz)}
    z_before = {"gz": lax.rem(gz + ngz - 1, ngz)}
    diagonals = [{**t_side, **z_side} for t_side in (t_before, t_after) for z_side in (z_before, z_after)]

    loads = {}
    for index, (name, source, target) in enumerate((
        ("rhs", rhs_hbm, rhs_ref), ("smoother", smoother_hbm, smoother_ref),
        ("weights", weight_hbm, weight_ref), ("blocks", blocks_hbm, blocks_ref),
        ("next", next_hbm, next_ref), ("aggregate", aggregate_hbm, aggregate_ref),
        ("restrict", restrict_hbm, restrict_ref), ("prolong", prolong_hbm, prolong_ref),
        ("coarse", coarse_hbm, coarse_ref),
        ("coarse_smoother", coarse_smoother_hbm, coarse_smoother_ref),
        ("coarse_next", coarse_next_hbm, coarse_next_ref),
    )):
        loads[name] = pltpu.make_async_copy(source, target, load_sem.at[index])
        loads[name].start()

    barrier = pltpu.get_barrier_semaphore()
    for device in [t_after, t_before, z_after, z_before] + diagonals:
        pl.semaphore_signal(barrier, inc=1, device_id=device, device_id_type=MESH)
    pl.semaphore_wait(barrier, 8)

    pending = []

    def send(number, index, source, target, device):
        copy = pltpu.make_async_remote_copy(
            src_ref=source,
            dst_ref=target,
            send_sem=send_sem.at[number, index],
            recv_sem=recv_sem.at[number, index],
            device_id=device,
            device_id_type=MESH,
        )
        copy.start()
        pending.append(copy)
        return copy

    def send_z(buffer, number, pad, width=1):
        inner = pl.ds(pad, nt)
        low, high = pl.ds(pad, width), pl.ds(pad + nz - width, width)
        above, below = pl.ds(pad + nz, width), pl.ds(pad - width, width)
        return [
            send(number, 0, buffer.at[inner, low], buffer.at[inner, above], z_before),
            send(number, 1, buffer.at[inner, high], buffer.at[inner, below], z_after),
        ]

    def send_t(buffer, number, pad, width=1):
        inner = pl.ds(pad, nz)
        low, high = pl.ds(pad, width), pl.ds(pad + nt - width, width)
        above, below = pl.ds(pad + nt, width), pl.ds(pad - width, width)
        return [
            send(number, 2, buffer.at[low, inner], buffer.at[above, inner], t_before),
            send(number, 3, buffer.at[high, inner], buffer.at[below, inner], t_after),
        ]

    def arrive(copies):
        for copy in copies:
            copy.wait_recv()

    rows = [[(t, z) for z in range(nz)] for t in range(nt)]
    columns = [[(t, z) for t in range(nt)] for z in range(nz)]
    edges_first = [0, nz - 1] + list(range(1, nz - 1))
    around = [
        [(-1, z) for z in range(nz)], [(nt, z) for z in range(nz)],
        [(t, -1) for t in range(nt)], [(t, nz) for t in range(nt)],
    ]
    steps = {1: (1, 0), 2: (-1, 0), 3: (0, 1), 4: (0, -1)}
    order = (0, 5, 6, 7, 8, 3, 4, 1, 2)
    down_order = order[:7] + (2,)

    def lanes(x, s):
        return x[:, s * plane:(s + 1) * plane]

    def image(source, places, pair, terms, local):
        own = [source[t + 2, z + 2] for t, z in places]
        if 5 in terms:
            moved = dot(jnp.concatenate([stacked(v, 1) for v in own], axis=0), shuffle[...])
        parts = []
        for k in terms:
            if k == 0:
                row = own
            elif k > 4:
                row = [
                    moved[s * cf:(s + 1) * cf, (k - 5) * plane:(k - 4) * plane]
                    * weights[t + 1, z + 1, k - 1:k]
                    for s, (t, z) in enumerate(places)
                ]
            else:
                dt, dz = steps[k]
                row = [
                    jnp.zeros((cf, plane), F32)
                    if local and not (0 <= t + dt < nt and 0 <= z + dz < nz)
                    else source[t + 2 + dt, z + 2 + dz] * weights[t + 1, z + 1, k - 1:k]
                    for t, z in places
                ]
            parts.append(jnp.concatenate(row, axis=1))
        wide = parts[0] if len(parts) == 1 else jnp.concatenate(parts, axis=0)
        return left_product(pair[...], wide)

    def less(base, target, places, wide):
        for s, (t, z) in enumerate(places):
            target[t + 2, z + 2] = base[t + 2, z + 2] - lanes(wide, s)

    def local_terms(form, source, base, target):
        for t, places in enumerate(rows):
            if t == 0:
                pair, terms = all_pairs.at[form, :, pl.ds(0, 8 * cf)], order[:8]
            elif t == nt - 1:
                pair, terms = down_pairs.at[form], down_order
            else:
                pair, terms = all_pairs.at[form], order
            less(base, target, places, image(source, places, pair, terms, True))

    def edge(form, source, target, k, places):
        wide = image(source, places, single_pairs.at[form, k - 1], (k,), False)
        less(target, target, places, wide)

    def t_edges(form, source, target):
        edge(form, source, target, 1, rows[-1])
        edge(form, source, target, 2, rows[0])

    def z_edges(form, source, target):
        edge(form, source, target, 4, columns[0])
        edge(form, source, target, 3, columns[-1])

    def all_terms(form, source, base, target, places):
        less(base, target, places, image(source, places, all_pairs.at[form], order, False))

    r0, r1, r2, r3, r4, r5, correction = [fields.at[index] for index in range(7)]
    loads["rhs"].wait()
    for z in edges_first:
        for t in range(nt):
            r0[t + 2, z + 2] = rhs_ref[pl.ds(t * nz + z, cf, stride=sites), :]
        if z == nz - 1:
            z_copies = send_z(r0, 0, 2)
    t_copies = send_t(r0, 0, 2)

    for name in ("smoother", "weights", "blocks", "next"):
        loads[name].wait()
    for t in range(nt):
        for z in range(nz):
            weights[t + 1, z + 1] = weight_ref[pl.ds(t * nz + z, 8, stride=sites), :]
    weight_copies = send_z(weights, 4, 1) + send_t(weights, 4, 1)
    smooth_pair[...] = stacked(smoother_ref[...], 0)
    blocks = [blocks_ref[k] for k in range(9)]
    smoothed = lax.dot_general(
        jnp.concatenate(blocks, axis=0), smoother_ref[...], NN,
        precision=lax.Precision.HIGHEST, preferred_element_type=F32,
    )
    smoothed = [smoothed[k * cf:(k + 1) * cf] for k in range(9)]
    for form, parts in enumerate((smoothed, blocks)):
        all_pairs[form] = stacked(jnp.concatenate([parts[k] for k in order], axis=1), 0)
        down_pairs[form] = stacked(jnp.concatenate([parts[k] for k in down_order], axis=1), 0)
        for k in range(1, 5):
            single_pairs[form, k - 1] = stacked(parts[k], 0)
    line = lax.broadcasted_iota(jnp.int32, (plane, plane), 0)
    for k in range(4):
        chosen = jnp.where(line == next_ref[k:k + 1, :], 1.0, 0.0).astype(BF16)
        shuffle[:, k * plane:(k + 1) * plane] = jnp.concatenate([chosen, chosen], axis=0)
    local_terms(0, r0, r0, r1)

    for name in (
        "aggregate", "restrict", "prolong", "coarse", "coarse_smoother", "coarse_next"
    ):
        loads[name].wait()
    crows = sites * cplane
    line = lax.broadcasted_iota(jnp.int32, (crows, plane), 0)
    for s in range(sites):
        chosen = jnp.where(line == aggregate_ref[...] + s * cplane, 1.0, 0.0).astype(BF16)
        spread[:, s * plane:(s + 1) * plane] = jnp.concatenate([chosen, chosen], axis=0)
    restrict_pair[...] = stacked(restrict_ref[...], 1)
    prolong_pair[...] = stacked(prolong_ref[...], 0)
    coarse_near[...] = stacked(
        jnp.concatenate([jnp.transpose(coarse_ref[k]) for k in (0, 5, 6, 7, 8)], axis=0), 1
    )
    coarse_hop[...] = stacked(
        jnp.concatenate([jnp.transpose(coarse_ref[k]) for k in (1, 2, 3, 4)], axis=0), 1
    )
    coarse_smooth[...] = stacked(jnp.transpose(coarse_smoother_ref[...]), 1)
    column = lax.broadcasted_iota(jnp.int32, (cplane, crows), 1)
    within = lax.rem(column, cplane)
    tiling = jnp.where(lax.broadcasted_iota(jnp.int32, (cplane, crows), 0) == within, 1.0, 0.0)
    padded_next = jnp.concatenate(
        [coarse_next_ref[...].astype(F32), jnp.zeros((4, cplane), F32)], axis=0
    )
    targets = dot(padded_next.astype(BF16), tiling.astype(BF16))
    line = lax.broadcasted_iota(jnp.int32, (crows, crows), 0).astype(F32)
    column = lax.broadcasted_iota(jnp.int32, (crows, crows), 1)
    start = (column - lax.rem(column, cplane)).astype(F32)
    for k, opposite in enumerate((1, 0, 3, 2)):
        chosen = jnp.where(line == start + targets[opposite:opposite + 1, :], 1.0, 0.0)
        chosen = chosen.astype(BF16)
        coarse_shuffle[k * crows:(k + 1) * crows, :] = jnp.concatenate([chosen, chosen], axis=1)

    arrive(t_copies)
    t_edges(0, r0, r1)
    arrive(z_copies)
    z_edges(0, r0, r1)
    z_copies = send_z(r1, 1, 2)
    t_copies = send_t(r1, 1, 2)
    local_terms(0, r1, r1, r2)
    arrive(t_copies)
    t_edges(0, r1, r2)
    arrive(z_copies)
    z_edges(0, r1, r2)

    rest_copies = send_z(r2, 2, 2) + send_t(r2, 2, 2)

    line = lax.broadcasted_iota(jnp.int32, (2 * cplane, plane), 0)
    gather = jnp.where(line == aggregate_ref[...], 1.0, 0.0).astype(BF16)
    gather = jnp.concatenate([gather, gather], axis=1)
    sums = [
        dot(gather, stacked(r2[t + 2, z + 2], 1), NT)[:cplane]
        for t in range(nt) for z in range(nz)
    ]
    coarse_rhs[...] = right_product(jnp.concatenate(sums, axis=0), restrict_pair[...])

    def put(buffer, flat):
        for t in range(nt):
            for z in range(nz):
                s = t * nz + z
                buffer[t + 2, z + 2] = flat[s * cplane:(s + 1) * cplane]

    def shifted(buffer, dt, dz):
        return jnp.concatenate(
            [buffer[t + 2 + dt, z + 2 + dz] for t in range(nt) for z in range(nz)], axis=0
        )

    current = right_product(coarse_rhs[...], coarse_smooth[...])
    for sweep in range(SWEEPS):
        buffer = values.at[sweep]
        put(buffer, current)
        copies = send_z(buffer, 5 + sweep, 2) + send_t(buffer, 5 + sweep, 2)
        moved = dot(coarse_shuffle[...], stacked(current, 0))
        terms = [current] + [moved[k * crows:(k + 1) * crows] for k in range(4)]
        rest_coarse = coarse_rhs[...] - right_product(
            jnp.concatenate(terms, axis=1), coarse_near[...]
        )
        arrive(copies)
        terms = [shifted(buffer, dt, dz) for dt, dz in steps.values()]
        rest_coarse -= right_product(jnp.concatenate(terms, axis=1), coarse_hop[...])
        current += right_product(rest_coarse, coarse_smooth[...])
    buffer = values.at[SWEEPS]
    put(buffer, current)
    number = 5 + SWEEPS
    copies = send_z(buffer, number, 2, 2) + send_t(buffer, number, 2, 2)
    sides = [(t, z) for t in (0, 1) for z in (0, 1)]
    for index, (device, (t, z)) in enumerate(zip(diagonals, sides)):
        source = buffer.at[1 + nt if t else 2, 1 + nz if z else 2]
        target = buffer.at[1 if t else 2 + nt, 1 if z else 2 + nz]
        copies.append(send(number, 4 + index, source, target, device))

    def prolong(flat, places):
        lifted = stacked(left_product(prolong_pair[...], flat, NT), 1)
        wide = dot(lifted, spread[...])
        for s, (t, z) in enumerate(places):
            correction[t + 2, z + 2] = lanes(wide, s)

    prolong(current, [place for places in rows for place in places])
    local_terms(1, correction, r2, r3)
    arrive(copies)
    halo = [place for places in around for place in places]
    halo += [(t, z) for t in (-2, nt + 1) for z in range(nz)]
    halo += [(t, z) for t in range(nt) for z in (-2, nz + 1)]
    halo += [(t, z) for t in (-1, nt) for z in (-1, nz)]
    for begin in range(0, len(halo), sites):
        places = halo[begin:begin + sites]
        flat = [buffer[t + 2, z + 2] for t, z in places]
        flat += [jnp.zeros((cplane, cc), F32)] * (sites - len(places))
        prolong(jnp.concatenate(flat, axis=0), places)
    t_edges(1, correction, r3)
    z_edges(1, correction, r3)
    arrive(weight_copies)
    arrive(rest_copies)
    for places in around:
        all_terms(1, correction, r2, r3, places)

    for z in edges_first:
        all_terms(0, r3, r3, r4, columns[z])
        if z == nz - 1:
            z_copies = send_z(r4, 3, 2)
    t_copies = send_t(r4, 3, 2)
    local_terms(0, r4, r4, r5)
    for places in rows:
        wide = jnp.concatenate([
            r0[t + 2, z + 2] + r1[t + 2, z + 2] + r3[t + 2, z + 2] + r4[t + 2, z + 2]
            for t, z in places
        ], axis=1)
        wide = left_product(smooth_pair[...], wide)
        for s, (t, z) in enumerate(places):
            solution_ref[pl.ds(t * nz + z, cf, stride=sites), :] = (
                correction[t + 2, z + 2] + lanes(wide, s)
            )
    arrive(t_copies)
    t_edges(0, r4, r5)
    for places in columns[1:-1]:
        for t, z in places:
            residual_ref[pl.ds(t * nz + z, cf, stride=sites), :] = r5[t + 2, z + 2]
    arrive(z_copies)
    z_edges(0, r4, r5)
    for places in (columns[0], columns[-1]):
        for t, z in places:
            residual_ref[pl.ds(t * nz + z, cf, stride=sites), :] = r5[t + 2, z + 2]
    for copy in pending:
        copy.wait_send()


def solution(mesh):
    def shards(
        rhs_field, link_weights, fine_blocks, smoother, plane_next, aggregate,
        restrict_map, prolong_map, coarse_blocks, coarse_smoother, coarse_next,
    ):
        _, cf, nt, nz, plane = rhs_field.shape
        cplane = coarse_next.shape[1]
        cc = coarse_smoother.shape[0]
        sites = nt * nz
        crows = sites * cplane
        sizes = (
            nt, nz, cf, plane, cplane, cc,
            mesh.shape["col"], mesh.shape["ta"], mesh.shape["gz"],
        )
        out = jax.ShapeDtypeStruct((cf * sites, plane), F32)
        vmem = pl.BlockSpec(memory_space=pltpu.VMEM)
        hbm = pl.BlockSpec(memory_space=pltpu.HBM)
        operands = (
            rhs_field.reshape(cf * sites, plane), link_weights.reshape(-1, plane), fine_blocks,
            smoother, plane_next, aggregate.reshape(1, plane), restrict_map, prolong_map.T,
            coarse_blocks, coarse_smoother, coarse_next,
        )
        solved, residual = pl.pallas_call(
            functools.partial(kernel, sizes),
            out_shape=(out, out),
            in_specs=[hbm] * len(operands),
            out_specs=(vmem, vmem),
            scratch_shapes=[pltpu.VMEM(operand.shape, operand.dtype) for operand in operands] + [
                pltpu.VMEM((7, nt + 4, nz + 4, cf, plane), F32),
                pltpu.VMEM((1 + SWEEPS, nt + 4, nz + 4, cplane, cc), F32),
                pltpu.VMEM((nt + 2, nz + 2, 8, plane), F32),
                pltpu.VMEM((crows, cc), F32),
                pltpu.VMEM((2, 2 * cf, 9 * cf), BF16),
                pltpu.VMEM((2, 2 * cf, 8 * cf), BF16),
                pltpu.VMEM((2, 4, 2 * cf, cf), BF16),
                pltpu.VMEM((2 * cf, cf), BF16),
                pltpu.VMEM((2 * plane, 4 * plane), BF16),
                pltpu.VMEM((2 * crows, sites * plane), BF16),
                pltpu.VMEM((cf, 2 * cc), BF16),
                pltpu.VMEM((2 * cf, cc), BF16),
                pltpu.VMEM((5 * cc, 2 * cc), BF16),
                pltpu.VMEM((4 * cc, 2 * cc), BF16),
                pltpu.VMEM((cc, 2 * cc), BF16),
                pltpu.VMEM((4 * crows, 2 * crows), BF16),
                pltpu.SemaphoreType.DMA((len(operands),)),
                pltpu.SemaphoreType.DMA((6 + SWEEPS, 8)),
                pltpu.SemaphoreType.DMA((6 + SWEEPS, 8)),
            ],
            compiler_params=pltpu.CompilerParams(
                collective_id=0, has_side_effects=True, vmem_limit_bytes=63 * 1024 * 1024
            ),
        )(*operands)
        return solved.reshape(rhs_field.shape), residual.reshape(rhs_field.shape)

    return jax.shard_map(
        shards,
        mesh=mesh,
        in_specs=(
            P(None, None, ("ta", "col"), "gz", None),
            P(None, ("ta", "col"), "gz", None),
            P(), P(), P(), P(), P(), P(), P(), P(), P(),
        ),
        out_specs=(
            P(None, None, ("ta", "col"), "gz", None),
            P(None, None, ("ta", "col"), "gz", None),
        ),
        check_vma=False,
    )
```

```python
import functools

import jax
import jax.numpy as jnp
from jax import lax
from jax.experimental import pallas as pl
from jax.experimental.pallas import tpu as pltpu
from jax.sharding import PartitionSpec as P

SWEEPS = 3
F32 = jnp.float32
BF16 = jnp.bfloat16
MESH = pl.DeviceIdType.MESH
NN = (((1,), (0,)), ((), ()))
NT = (((1,), (1,)), ((), ()))


def dot(a, b, dims=NN):
    return lax.dot_general(a, b, dims, preferred_element_type=F32)


def split(x):
    hi = x.astype(BF16)
    return hi, (x - hi.astype(F32)).astype(BF16)


def stacked(x, axis):
    return jnp.concatenate(split(x), axis=axis)


def left_product(pair, x, dims=NN):
    rows = pair.shape[0] // 2
    hi, lo = split(x)
    both = dot(pair, hi, dims)
    return both[:rows] + both[rows:] + dot(pair[:rows], lo, dims)


def right_product(x, pair):
    columns = pair.shape[1] // 2
    hi, lo = split(x)
    both = dot(hi, pair)
    return both[:, :columns] + both[:, columns:] + dot(lo, pair[:, :columns])


def kernel(
    sizes,
    rhs_hbm, weight_hbm, blocks_hbm, smoother_hbm, next_hbm, aggregate_hbm,
    restrict_hbm, prolong_hbm, coarse_hbm, coarse_smoother_hbm, coarse_next_hbm,
    solution_ref, residual_ref,
    rhs_ref, weight_ref, blocks_ref, smoother_ref, next_ref, aggregate_ref,
    restrict_ref, prolong_ref, coarse_ref, coarse_smoother_ref, coarse_next_ref,
    fields, values, weights, coarse_rhs,
    all_pairs, down_pairs, single_pairs, smooth_pair, shuffle, spread,
    restrict_pair, prolong_pair, coarse_near, coarse_hop, coarse_smooth, coarse_shuffle,
    load_sem, send_sem, recv_sem,
):
    nt, nz, cf, plane, cplane, cc, ncol, nta, ngz = sizes
    sites = nt * nz
    ta, gz, col = lax.axis_index("ta"), lax.axis_index("gz"), lax.axis_index("col")
    ring = nta * ncol
    here = ta * ncol + col
    after, before = lax.rem(here + 1, ring), lax.rem(here + ring - 1, ring)
    t_after = {"ta": after // ncol, "col": lax.rem(after, ncol)}
    t_before = {"ta": before // ncol, "col": lax.rem(before, ncol)}
    z_after = {"gz": lax.rem(gz + 1, ngz)}
    z_before = {"gz": lax.rem(gz + ngz - 1, ngz)}
    diagonals = [{**t_side, **z_side} for t_side in (t_before, t_after) for z_side in (z_before, z_after)]

    loads = {}
    for index, (name, source, target) in enumerate((
        ("rhs", rhs_hbm, rhs_ref), ("smoother", smoother_hbm, smoother_ref),
        ("weights", weight_hbm, weight_ref), ("blocks", blocks_hbm, blocks_ref),
        ("next", next_hbm, next_ref), ("aggregate", aggregate_hbm, aggregate_ref),
        ("restrict", restrict_hbm, restrict_ref), ("prolong", prolong_hbm, prolong_ref),
        ("coarse", coarse_hbm, coarse_ref),
        ("coarse_smoother", coarse_smoother_hbm, coarse_smoother_ref),
        ("coarse_next", coarse_next_hbm, coarse_next_ref),
    )):
        loads[name] = pltpu.make_async_copy(source, target, load_sem.at[index])
        loads[name].start()

    barrier = pltpu.get_barrier_semaphore()
    for device in [t_after, t_before, z_after, z_before] + diagonals:
        pl.semaphore_signal(barrier, inc=1, device_id=device, device_id_type=MESH)
    pl.semaphore_wait(barrier, 8)

    pending = []

    def send(number, index, source, target, device):
        copy = pltpu.make_async_remote_copy(
            src_ref=source,
            dst_ref=target,
            send_sem=send_sem.at[number, index],
            recv_sem=recv_sem.at[number, index],
            device_id=device,
            device_id_type=MESH,
        )
        copy.start()
        pending.append(copy)
        return copy

    def send_low(buffer, number, pad, width=1):
        inner, low, above = pl.ds(pad, nt), pl.ds(pad, width), pl.ds(pad + nz, width)
        return [send(number, 0, buffer.at[inner, low], buffer.at[inner, above], z_before)]

    def send_high(buffer, number, pad, width=1):
        inner, high, below = pl.ds(pad, nt), pl.ds(pad + nz - width, width), pl.ds(pad - width, width)
        return [send(number, 1, buffer.at[inner, high], buffer.at[inner, below], z_after)]

    def send_z(buffer, number, pad, width=1):
        return send_low(buffer, number, pad, width) + send_high(buffer, number, pad, width)

    def send_t(buffer, number, pad, width=1):
        inner = pl.ds(pad, nz)
        low, high = pl.ds(pad, width), pl.ds(pad + nt - width, width)
        above, below = pl.ds(pad + nt, width), pl.ds(pad - width, width)
        return [
            send(number, 2, buffer.at[low, inner], buffer.at[above, inner], t_before),
            send(number, 3, buffer.at[high, inner], buffer.at[below, inner], t_after),
        ]

    def arrive(copies):
        for copy in copies:
            copy.wait_recv()

    rows = [[(t, z) for z in range(nz)] for t in range(nt)]
    columns = [[(t, z) for t in range(nt)] for z in range(nz)]
    edges_first = [0, nz - 1] + list(range(1, nz - 1))
    around = [
        [(-1, z) for z in range(nz)], [(nt, z) for z in range(nz)],
        [(t, -1) for t in range(nt)], [(t, nz) for t in range(nt)],
    ]
    steps = {1: (1, 0), 2: (-1, 0), 3: (0, 1), 4: (0, -1)}
    order = (0, 5, 6, 7, 8, 3, 4, 1, 2)
    down_order = order[:7] + (2,)

    def lanes(x, s):
        return x[:, s * plane:(s + 1) * plane]

    def image(source, places, pair, terms, local):
        own = [source[t + 2, z + 2] for t, z in places]
        if 5 in terms:
            moved = dot(jnp.concatenate([stacked(v, 1) for v in own], axis=0), shuffle[...])
        parts = []
        for k in terms:
            if k == 0:
                row = own
            elif k > 4:
                row = [
                    moved[s * cf:(s + 1) * cf, (k - 5) * plane:(k - 4) * plane]
                    * weights[t + 1, z + 1, k - 1:k]
                    for s, (t, z) in enumerate(places)
                ]
            else:
                dt, dz = steps[k]
                row = [
                    jnp.zeros((cf, plane), F32)
                    if local and not (0 <= t + dt < nt and 0 <= z + dz < nz)
                    else source[t + 2 + dt, z + 2 + dz] * weights[t + 1, z + 1, k - 1:k]
                    for t, z in places
                ]
            parts.append(jnp.concatenate(row, axis=1))
        wide = parts[0] if len(parts) == 1 else jnp.concatenate(parts, axis=0)
        return left_product(pair[...], wide)

    def less(base, target, places, wide):
        for s, (t, z) in enumerate(places):
            target[t + 2, z + 2] = base[t + 2, z + 2] - lanes(wide, s)

    def local_terms(form, source, base, target):
        for t, places in enumerate(rows):
            if t == 0:
                pair, terms = all_pairs.at[form, :, pl.ds(0, 8 * cf)], order[:8]
            elif t == nt - 1:
                pair, terms = down_pairs.at[form], down_order
            else:
                pair, terms = all_pairs.at[form], order
            less(base, target, places, image(source, places, pair, terms, True))

    def edge(form, source, target, k, places):
        wide = image(source, places, single_pairs.at[form, k - 1], (k,), False)
        less(target, target, places, wide)

    def t_edges(form, source, target):
        edge(form, source, target, 1, rows[-1])
        edge(form, source, target, 2, rows[0])

    def z_edges(form, source, target):
        edge(form, source, target, 4, columns[0])
        edge(form, source, target, 3, columns[-1])

    def all_terms(form, source, base, target, places):
        less(base, target, places, image(source, places, all_pairs.at[form], order, False))

    r0, r1, r2, r3, r4, r5, correction = [fields.at[index] for index in range(7)]
    loads["rhs"].wait()
    for z in edges_first:
        for t in range(nt):
            r0[t + 2, z + 2] = rhs_ref[pl.ds(t * nz + z, cf, stride=sites), :]
        if z == 0:
            z_copies = send_low(r0, 0, 2)
        if z == nz - 1:
            z_copies += send_high(r0, 0, 2)
    t_copies = send_t(r0, 0, 2)

    for name in ("smoother", "weights", "blocks", "next"):
        loads[name].wait()
    for t in range(nt):
        for z in range(nz):
            weights[t + 1, z + 1] = weight_ref[pl.ds(t * nz + z, 8, stride=sites), :]
    smooth_pair[...] = stacked(smoother_ref[...], 0)
    blocks = [blocks_ref[k] for k in range(9)]
    smoothed = lax.dot_general(
        jnp.concatenate(blocks, axis=0), smoother_ref[...], NN,
        precision=lax.Precision.HIGHEST, preferred_element_type=F32,
    )
    smoothed = [smoothed[k * cf:(k + 1) * cf] for k in range(9)]
    for form, parts in enumerate((smoothed, blocks)):
        all_pairs[form] = stacked(jnp.concatenate([parts[k] for k in order], axis=1), 0)
        down_pairs[form] = stacked(jnp.concatenate([parts[k] for k in down_order], axis=1), 0)
        for k in range(1, 5):
            single_pairs[form, k - 1] = stacked(parts[k], 0)
    line = lax.broadcasted_iota(jnp.int32, (plane, plane), 0)
    for k in range(4):
        chosen = jnp.where(line == next_ref[k:k + 1, :], 1.0, 0.0).astype(BF16)
        shuffle[:, k * plane:(k + 1) * plane] = jnp.concatenate([chosen, chosen], axis=0)
    local_terms(0, r0, r0, r1)

    for name in (
        "aggregate", "restrict", "prolong", "coarse", "coarse_smoother", "coarse_next"
    ):
        loads[name].wait()
    crows = sites * cplane
    line = lax.broadcasted_iota(jnp.int32, (crows, plane), 0)
    for s in range(sites):
        chosen = jnp.where(line == aggregate_ref[...] + s * cplane, 1.0, 0.0).astype(BF16)
        spread[:, s * plane:(s + 1) * plane] = jnp.concatenate([chosen, chosen], axis=0)
    restrict_pair[...] = stacked(restrict_ref[...], 1)
    prolong_pair[...] = stacked(prolong_ref[...], 0)
    coarse_near[...] = stacked(
        jnp.concatenate([jnp.transpose(coarse_ref[k]) for k in (0, 5, 6, 7, 8)], axis=0), 1
    )
    coarse_hop[...] = stacked(
        jnp.concatenate([jnp.transpose(coarse_ref[k]) for k in (1, 2, 3, 4)], axis=0), 1
    )
    coarse_smooth[...] = stacked(jnp.transpose(coarse_smoother_ref[...]), 1)
    column = lax.broadcasted_iota(jnp.int32, (cplane, crows), 1)
    within = lax.rem(column, cplane)
    tiling = jnp.where(lax.broadcasted_iota(jnp.int32, (cplane, crows), 0) == within, 1.0, 0.0)
    padded_next = jnp.concatenate(
        [coarse_next_ref[...].astype(F32), jnp.zeros((4, cplane), F32)], axis=0
    )
    targets = dot(padded_next.astype(BF16), tiling.astype(BF16))
    line = lax.broadcasted_iota(jnp.int32, (crows, crows), 0).astype(F32)
    column = lax.broadcasted_iota(jnp.int32, (crows, crows), 1)
    start = (column - lax.rem(column, cplane)).astype(F32)
    for k, opposite in enumerate((1, 0, 3, 2)):
        chosen = jnp.where(line == start + targets[opposite:opposite + 1, :], 1.0, 0.0)
        chosen = chosen.astype(BF16)
        coarse_shuffle[k * crows:(k + 1) * crows, :] = jnp.concatenate([chosen, chosen], axis=1)

    arrive(t_copies)
    t_edges(0, r0, r1)
    arrive(z_copies)
    edge(0, r0, r1, 4, columns[0])
    z_copies = send_low(r1, 1, 2)
    edge(0, r0, r1, 3, columns[-1])
    z_copies += send_high(r1, 1, 2)
    t_copies = send_t(r1, 1, 2)
    local_terms(0, r1, r1, r2)
    arrive(t_copies)
    t_edges(0, r1, r2)
    arrive(z_copies)
    z_edges(0, r1, r2)

    pieces = 1 + SWEEPS

    def send_piece(piece):
        number = 6 + SWEEPS + piece
        copies = []
        for count, build in ((nt, lambda part: (
            (0, (part, 2), (part, 2 + nz), z_before), (1, (part, 1 + nz), (part, 1), z_after),
        )), (nz, lambda part: (
            (2, (2, part), (2 + nt, part), t_before), (3, (1 + nt, part), (1, part), t_after),
        ))):
            begin, end = count * piece // pieces, count * (piece + 1) // pieces
            if begin < end:
                for index, source, target, device in build(pl.ds(2 + begin, end - begin)):
                    copies.append(send(number, index, r2.at[source], r2.at[target], device))
        return copies

    rest_copies = send_piece(0)
    weight_copies = send_z(weights, 4, 1) + send_t(weights, 4, 1)

    line = lax.broadcasted_iota(jnp.int32, (2 * cplane, plane), 0)
    gather = jnp.where(line == aggregate_ref[...], 1.0, 0.0).astype(BF16)
    gather = jnp.concatenate([gather, gather], axis=1)
    sums = [
        dot(gather, stacked(r2[t + 2, z + 2], 1), NT)[:cplane]
        for t in range(nt) for z in range(nz)
    ]
    coarse_rhs[...] = right_product(jnp.concatenate(sums, axis=0), restrict_pair[...])

    def put(buffer, flat):
        for t in range(nt):
            for z in range(nz):
                s = t * nz + z
                buffer[t + 2, z + 2] = flat[s * cplane:(s + 1) * cplane]

    def shifted(buffer, dt, dz):
        return jnp.concatenate(
            [buffer[t + 2 + dt, z + 2 + dz] for t in range(nt) for z in range(nz)], axis=0
        )

    current = right_product(coarse_rhs[...], coarse_smooth[...])
    for sweep in range(SWEEPS):
        buffer = values.at[sweep]
        put(buffer, current)
        copies = send_z(buffer, 5 + sweep, 2) + send_t(buffer, 5 + sweep, 2)
        rest_copies += send_piece(1 + sweep)
        moved = dot(coarse_shuffle[...], stacked(current, 0))
        terms = [current] + [moved[k * crows:(k + 1) * crows] for k in range(4)]
        rest_coarse = coarse_rhs[...] - right_product(
            jnp.concatenate(terms, axis=1), coarse_near[...]
        )
        arrive(copies)
        terms = [shifted(buffer, dt, dz) for dt, dz in steps.values()]
        rest_coarse -= right_product(jnp.concatenate(terms, axis=1), coarse_hop[...])
        current += right_product(rest_coarse, coarse_smooth[...])
    buffer = values.at[SWEEPS]
    put(buffer, current)
    number = 5 + SWEEPS
    copies = send_z(buffer, number, 2, 2) + send_t(buffer, number, 2, 2)
    sides = [(t, z) for t in (0, 1) for z in (0, 1)]
    for index, (device, (t, z)) in enumerate(zip(diagonals, sides)):
        source = buffer.at[1 + nt if t else 2, 1 + nz if z else 2]
        target = buffer.at[1 if t else 2 + nt, 1 if z else 2 + nz]
        copies.append(send(number, 4 + index, source, target, device))

    def prolong(flat, places):
        lifted = stacked(left_product(prolong_pair[...], flat, NT), 1)
        wide = dot(lifted, spread[...])
        for s, (t, z) in enumerate(places):
            correction[t + 2, z + 2] = lanes(wide, s)

    prolong(current, [place for places in rows for place in places])
    local_terms(1, correction, r2, r3)
    arrive(copies)
    halo = [place for places in around for place in places]
    halo += [(t, z) for t in (-2, nt + 1) for z in range(nz)]
    halo += [(t, z) for t in range(nt) for z in (-2, nz + 1)]
    halo += [(t, z) for t in (-1, nt) for z in (-1, nz)]
    for begin in range(0, len(halo), sites):
        places = halo[begin:begin + sites]
        flat = [buffer[t + 2, z + 2] for t, z in places]
        flat += [jnp.zeros((cplane, cc), F32)] * (sites - len(places))
        prolong(jnp.concatenate(flat, axis=0), places)
    t_edges(1, correction, r3)
    z_edges(1, correction, r3)
    arrive(weight_copies)
    arrive(rest_copies)
    for places in around:
        all_terms(1, correction, r2, r3, places)

    for z in edges_first:
        all_terms(0, r3, r3, r4, columns[z])
        if z == 0:
            z_copies = send_low(r4, 3, 2)
        if z == nz - 1:
            z_copies += send_high(r4, 3, 2)
    t_copies = send_t(r4, 3, 2)
    local_terms(0, r4, r4, r5)
    for places in rows:
        wide = jnp.concatenate([
            r0[t + 2, z + 2] + r1[t + 2, z + 2] + r3[t + 2, z + 2] + r4[t + 2, z + 2]
            for t, z in places
        ], axis=1)
        wide = left_product(smooth_pair[...], wide)
        for s, (t, z) in enumerate(places):
            solution_ref[pl.ds(t * nz + z, cf, stride=sites), :] = (
                correction[t + 2, z + 2] + lanes(wide, s)
            )
    arrive(t_copies)
    t_edges(0, r4, r5)
    for places in columns[1:-1]:
        for t, z in places:
            residual_ref[pl.ds(t * nz + z, cf, stride=sites), :] = r5[t + 2, z + 2]
    arrive(z_copies)
    z_edges(0, r4, r5)
    for places in (columns[0], columns[-1]):
        for t, z in places:
            residual_ref[pl.ds(t * nz + z, cf, stride=sites), :] = r5[t + 2, z + 2]
    for copy in pending:
        copy.wait_send()


def solution(mesh):
    def shards(
        rhs_field, link_weights, fine_blocks, smoother, plane_next, aggregate,
        restrict_map, prolong_map, coarse_blocks, coarse_smoother, coarse_next,
    ):
        _, cf, nt, nz, plane = rhs_field.shape
        cplane = coarse_next.shape[1]
        cc = coarse_smoother.shape[0]
        sites = nt * nz
        crows = sites * cplane
        sizes = (
            nt, nz, cf, plane, cplane, cc,
            mesh.shape["col"], mesh.shape["ta"], mesh.shape["gz"],
        )
        out = jax.ShapeDtypeStruct((cf * sites, plane), F32)
        vmem = pl.BlockSpec(memory_space=pltpu.VMEM)
        hbm = pl.BlockSpec(memory_space=pltpu.HBM)
        operands = (
            rhs_field.reshape(cf * sites, plane), link_weights.reshape(-1, plane), fine_blocks,
            smoother, plane_next, aggregate.reshape(1, plane), restrict_map, prolong_map.T,
            coarse_blocks, coarse_smoother, coarse_next,
        )
        solved, residual = pl.pallas_call(
            functools.partial(kernel, sizes),
            out_shape=(out, out),
            in_specs=[hbm] * len(operands),
            out_specs=(vmem, vmem),
            scratch_shapes=[pltpu.VMEM(operand.shape, operand.dtype) for operand in operands] + [
                pltpu.VMEM((7, nt + 4, nz + 4, cf, plane), F32),
                pltpu.VMEM((1 + SWEEPS, nt + 4, nz + 4, cplane, cc), F32),
                pltpu.VMEM((nt + 2, nz + 2, 8, plane), F32),
                pltpu.VMEM((crows, cc), F32),
                pltpu.VMEM((2, 2 * cf, 9 * cf), BF16),
                pltpu.VMEM((2, 2 * cf, 8 * cf), BF16),
                pltpu.VMEM((2, 4, 2 * cf, cf), BF16),
                pltpu.VMEM((2 * cf, cf), BF16),
                pltpu.VMEM((2 * plane, 4 * plane), BF16),
                pltpu.VMEM((2 * crows, sites * plane), BF16),
                pltpu.VMEM((cf, 2 * cc), BF16),
                pltpu.VMEM((2 * cf, cc), BF16),
                pltpu.VMEM((5 * cc, 2 * cc), BF16),
                pltpu.VMEM((4 * cc, 2 * cc), BF16),
                pltpu.VMEM((cc, 2 * cc), BF16),
                pltpu.VMEM((4 * crows, 2 * crows), BF16),
                pltpu.SemaphoreType.DMA((len(operands),)),
                pltpu.SemaphoreType.DMA((7 + 2 * SWEEPS, 8)),
                pltpu.SemaphoreType.DMA((7 + 2 * SWEEPS, 8)),
            ],
            compiler_params=pltpu.CompilerParams(
                collective_id=0, has_side_effects=True, vmem_limit_bytes=63 * 1024 * 1024
            ),
        )(*operands)
        return solved.reshape(rhs_field.shape), residual.reshape(rhs_field.shape)

    return jax.shard_map(
        shards,
        mesh=mesh,
        in_specs=(
            P(None, None, ("ta", "col"), "gz", None),
            P(None, ("ta", "col"), "gz", None),
            P(), P(), P(), P(), P(), P(), P(), P(), P(),
        ),
        out_specs=(
            P(None, None, ("ta", "col"), "gz", None),
            P(None, None, ("ta", "col"), "gz", None),
        ),
        check_vma=False,
    )
```

```python
import functools

import jax
import jax.numpy as jnp
from jax import lax
from jax.experimental import pallas as pl
from jax.experimental.pallas import tpu as pltpu
from jax.sharding import PartitionSpec as P

SWEEPS = 3
F32 = jnp.float32
BF16 = jnp.bfloat16
MESH = pl.DeviceIdType.MESH
NN = (((1,), (0,)), ((), ()))
NT = (((1,), (1,)), ((), ()))


def dot(a, b, dims=NN):
    return lax.dot_general(a, b, dims, preferred_element_type=F32)


def split(x):
    hi = x.astype(BF16)
    return hi, (x - hi.astype(F32)).astype(BF16)


def stacked(x, axis):
    return jnp.concatenate(split(x), axis=axis)


def left_product(pair, x, dims=NN):
    rows = pair.shape[0] // 2
    hi, lo = split(x)
    both = dot(pair, hi, dims)
    return both[:rows] + both[rows:] + dot(pair[:rows], lo, dims)


def right_product(x, pair):
    columns = pair.shape[1] // 2
    hi, lo = split(x)
    both = dot(hi, pair)
    return both[:, :columns] + both[:, columns:] + dot(lo, pair[:, :columns])


def kernel(
    sizes,
    rhs_hbm, weight_hbm, blocks_hbm, smoother_hbm, next_hbm, aggregate_hbm,
    restrict_hbm, prolong_hbm, coarse_hbm, coarse_smoother_hbm, coarse_next_hbm,
    solution_ref, residual_ref,
    rhs_ref, weight_ref, blocks_ref, smoother_ref, next_ref, aggregate_ref,
    restrict_ref, prolong_ref, coarse_ref, coarse_smoother_ref, coarse_next_ref,
    fields, values, weights, coarse_rhs,
    all_pairs, down_pairs, single_pairs, smooth_pair, shuffle, spread,
    restrict_pair, prolong_pair, coarse_near, coarse_hop, coarse_smooth, coarse_shuffle,
    load_sem, send_sem, recv_sem,
):
    nt, nz, cf, plane, cplane, cc, ncol, nta, ngz = sizes
    sites = nt * nz
    ta, gz, col = lax.axis_index("ta"), lax.axis_index("gz"), lax.axis_index("col")
    ring = nta * ncol
    here = ta * ncol + col
    after, before = lax.rem(here + 1, ring), lax.rem(here + ring - 1, ring)
    t_after = {"ta": after // ncol, "col": lax.rem(after, ncol)}
    t_before = {"ta": before // ncol, "col": lax.rem(before, ncol)}
    z_after = {"gz": lax.rem(gz + 1, ngz)}
    z_before = {"gz": lax.rem(gz + ngz - 1, ngz)}
    diagonals = [{**t_side, **z_side} for t_side in (t_before, t_after) for z_side in (z_before, z_after)]

    loads = {}
    for index, (name, source, target) in enumerate((
        ("rhs", rhs_hbm, rhs_ref), ("smoother", smoother_hbm, smoother_ref),
        ("weights", weight_hbm, weight_ref), ("blocks", blocks_hbm, blocks_ref),
        ("next", next_hbm, next_ref), ("aggregate", aggregate_hbm, aggregate_ref),
        ("restrict", restrict_hbm, restrict_ref), ("prolong", prolong_hbm, prolong_ref),
        ("coarse", coarse_hbm, coarse_ref),
        ("coarse_smoother", coarse_smoother_hbm, coarse_smoother_ref),
        ("coarse_next", coarse_next_hbm, coarse_next_ref),
    )):
        loads[name] = pltpu.make_async_copy(source, target, load_sem.at[index])
        loads[name].start()

    barrier = pltpu.get_barrier_semaphore()
    for device in [t_after, t_before, z_after, z_before] + diagonals:
        pl.semaphore_signal(barrier, inc=1, device_id=device, device_id_type=MESH)
    pl.semaphore_wait(barrier, 8)

    pending = []

    def send(number, index, source, target, device):
        copy = pltpu.make_async_remote_copy(
            src_ref=source,
            dst_ref=target,
            send_sem=send_sem.at[number, index],
            recv_sem=recv_sem.at[number, index],
            device_id=device,
            device_id_type=MESH,
        )
        copy.start()
        pending.append(copy)
        return copy

    def send_low(buffer, number, pad, width=1):
        inner, low, above = pl.ds(pad, nt), pl.ds(pad, width), pl.ds(pad + nz, width)
        return [send(number, 0, buffer.at[inner, low], buffer.at[inner, above], z_before)]

    def send_high(buffer, number, pad, width=1):
        inner, high, below = pl.ds(pad, nt), pl.ds(pad + nz - width, width), pl.ds(pad - width, width)
        return [send(number, 1, buffer.at[inner, high], buffer.at[inner, below], z_after)]

    def send_z(buffer, number, pad, width=1):
        return send_low(buffer, number, pad, width) + send_high(buffer, number, pad, width)

    def send_t(buffer, number, pad, width=1):
        inner = pl.ds(pad, nz)
        low, high = pl.ds(pad, width), pl.ds(pad + nt - width, width)
        above, below = pl.ds(pad + nt, width), pl.ds(pad - width, width)
        return [
            send(number, 2, buffer.at[low, inner], buffer.at[above, inner], t_before),
            send(number, 3, buffer.at[high, inner], buffer.at[below, inner], t_after),
        ]

    def arrive(copies):
        for copy in copies:
            copy.wait_recv()

    rows = [[(t, z) for z in range(nz)] for t in range(nt)]
    columns = [[(t, z) for t in range(nt)] for z in range(nz)]
    edges_first = [0, nz - 1] + list(range(1, nz - 1))
    around = [
        [(-1, z) for z in range(nz)], [(nt, z) for z in range(nz)],
        [(t, -1) for t in range(nt)], [(t, nz) for t in range(nt)],
    ]
    steps = {1: (1, 0), 2: (-1, 0), 3: (0, 1), 4: (0, -1)}
    order = (0, 5, 6, 7, 8, 3, 4, 1, 2)
    down_order = order[:7] + (2,)

    def lanes(x, s):
        return x[:, s * plane:(s + 1) * plane]

    def image(source, places, pair, terms, local):
        own = [source[t + 2, z + 2] for t, z in places]
        if 5 in terms:
            moved = dot(jnp.concatenate([stacked(v, 1) for v in own], axis=0), shuffle[...])
        parts = []
        for k in terms:
            if k == 0:
                row = own
            elif k > 4:
                row = [
                    moved[s * cf:(s + 1) * cf, (k - 5) * plane:(k - 4) * plane]
                    * weights[t + 1, z + 1, k - 1:k]
                    for s, (t, z) in enumerate(places)
                ]
            else:
                dt, dz = steps[k]
                row = [
                    jnp.zeros((cf, plane), F32)
                    if local and not (0 <= t + dt < nt and 0 <= z + dz < nz)
                    else source[t + 2 + dt, z + 2 + dz] * weights[t + 1, z + 1, k - 1:k]
                    for t, z in places
                ]
            parts.append(jnp.concatenate(row, axis=1))
        wide = parts[0] if len(parts) == 1 else jnp.concatenate(parts, axis=0)
        return left_product(pair[...], wide)

    def less(base, target, places, wide):
        for s, (t, z) in enumerate(places):
            target[t + 2, z + 2] = base[t + 2, z + 2] - lanes(wide, s)

    def local_terms(form, source, base, target):
        for t, places in enumerate(rows):
            if t == 0:
                pair, terms = all_pairs.at[form, :, pl.ds(0, 8 * cf)], order[:8]
            elif t == nt - 1:
                pair, terms = down_pairs.at[form], down_order
            else:
                pair, terms = all_pairs.at[form], order
            less(base, target, places, image(source, places, pair, terms, True))

    def edge(form, source, target, k, places):
        wide = image(source, places, single_pairs.at[form, k - 1], (k,), False)
        less(target, target, places, wide)

    def t_edges(form, source, target):
        edge(form, source, target, 1, rows[-1])
        edge(form, source, target, 2, rows[0])

    def z_edges(form, source, target):
        edge(form, source, target, 4, columns[0])
        edge(form, source, target, 3, columns[-1])

    def all_terms(form, source, base, target, places):
        less(base, target, places, image(source, places, all_pairs.at[form], order, False))

    r0, r1, r2, r3, r4, r5, correction = [fields.at[index] for index in range(7)]
    loads["rhs"].wait()
    for z in edges_first:
        for t in range(nt):
            r0[t + 2, z + 2] = rhs_ref[pl.ds(t * nz + z, cf, stride=sites), :]
        if z == 0:
            z_copies = send_low(r0, 0, 2)
        if z == nz - 1:
            z_copies += send_high(r0, 0, 2)
    t_copies = send_t(r0, 0, 2)

    for name in ("smoother", "weights", "blocks", "next"):
        loads[name].wait()
    for t in range(nt):
        for z in range(nz):
            weights[t + 1, z + 1] = weight_ref[pl.ds(t * nz + z, 8, stride=sites), :]
    smooth_pair[...] = stacked(smoother_ref[...], 0)
    blocks = [blocks_ref[k] for k in range(9)]
    smoothed = lax.dot_general(
        jnp.concatenate(blocks, axis=0), smoother_ref[...], NN,
        precision=lax.Precision.HIGHEST, preferred_element_type=F32,
    )
    smoothed = [smoothed[k * cf:(k + 1) * cf] for k in range(9)]
    for form, parts in enumerate((smoothed, blocks)):
        all_pairs[form] = stacked(jnp.concatenate([parts[k] for k in order], axis=1), 0)
        down_pairs[form] = stacked(jnp.concatenate([parts[k] for k in down_order], axis=1), 0)
        for k in range(1, 5):
            single_pairs[form, k - 1] = stacked(parts[k], 0)
    line = lax.broadcasted_iota(jnp.int32, (plane, plane), 0)
    for k in range(4):
        chosen = jnp.where(line == next_ref[k:k + 1, :], 1.0, 0.0).astype(BF16)
        shuffle[:, k * plane:(k + 1) * plane] = jnp.concatenate([chosen, chosen], axis=0)
    local_terms(0, r0, r0, r1)

    for name in (
        "aggregate", "restrict", "prolong", "coarse", "coarse_smoother", "coarse_next"
    ):
        loads[name].wait()
    crows = sites * cplane
    line = lax.broadcasted_iota(jnp.int32, (crows, plane), 0)
    for s in range(sites):
        chosen = jnp.where(line == aggregate_ref[...] + s * cplane, 1.0, 0.0).astype(BF16)
        spread[:, s * plane:(s + 1) * plane] = jnp.concatenate([chosen, chosen], axis=0)
    restrict_pair[...] = stacked(restrict_ref[...], 1)
    prolong_pair[...] = stacked(prolong_ref[...], 0)
    coarse_near[...] = stacked(
        jnp.concatenate([jnp.transpose(coarse_ref[k]) for k in (0, 5, 6, 7, 8)], axis=0), 1
    )
    coarse_hop[...] = stacked(
        jnp.concatenate([jnp.transpose(coarse_ref[k]) for k in (1, 2, 3, 4)], axis=0), 1
    )
    coarse_smooth[...] = stacked(jnp.transpose(coarse_smoother_ref[...]), 1)
    column = lax.broadcasted_iota(jnp.int32, (cplane, crows), 1)
    within = lax.rem(column, cplane)
    tiling = jnp.where(lax.broadcasted_iota(jnp.int32, (cplane, crows), 0) == within, 1.0, 0.0)
    padded_next = jnp.concatenate(
        [coarse_next_ref[...].astype(F32), jnp.zeros((4, cplane), F32)], axis=0
    )
    targets = dot(padded_next.astype(BF16), tiling.astype(BF16))
    line = lax.broadcasted_iota(jnp.int32, (crows, crows), 0).astype(F32)
    column = lax.broadcasted_iota(jnp.int32, (crows, crows), 1)
    start = (column - lax.rem(column, cplane)).astype(F32)
    for k, opposite in enumerate((1, 0, 3, 2)):
        chosen = jnp.where(line == start + targets[opposite:opposite + 1, :], 1.0, 0.0)
        chosen = chosen.astype(BF16)
        coarse_shuffle[k * crows:(k + 1) * crows, :] = jnp.concatenate([chosen, chosen], axis=1)

    arrive(t_copies)
    t_edges(0, r0, r1)
    arrive(z_copies)
    edge(0, r0, r1, 4, columns[0])
    z_copies = send_low(r1, 1, 2)
    edge(0, r0, r1, 3, columns[-1])
    z_copies += send_high(r1, 1, 2)
    t_copies = send_t(r1, 1, 2)
    weight_copies = send_z(weights, 4, 1) + send_t(weights, 4, 1)
    local_terms(0, r1, r1, r2)
    arrive(t_copies)
    t_edges(0, r1, r2)
    arrive(z_copies)
    z_edges(0, r1, r2)

    pieces = 1 + SWEEPS

    def send_piece(piece):
        number = 6 + SWEEPS + piece
        copies = []
        for count, build in ((nt, lambda part: (
            (0, (part, 2), (part, 2 + nz), z_before), (1, (part, 1 + nz), (part, 1), z_after),
        )), (nz, lambda part: (
            (2, (2, part), (2 + nt, part), t_before), (3, (1 + nt, part), (1, part), t_after),
        ))):
            begin, end = count * piece // pieces, count * (piece + 1) // pieces
            if begin < end:
                for index, source, target, device in build(pl.ds(2 + begin, end - begin)):
                    copies.append(send(number, index, r2.at[source], r2.at[target], device))
        return copies

    rest_copies = send_piece(0)

    line = lax.broadcasted_iota(jnp.int32, (2 * cplane, plane), 0)
    gather = jnp.where(line == aggregate_ref[...], 1.0, 0.0).astype(BF16)
    gather = jnp.concatenate([gather, gather], axis=1)
    sums = [
        dot(gather, stacked(r2[t + 2, z + 2], 1), NT)[:cplane]
        for t in range(nt) for z in range(nz)
    ]
    coarse_rhs[...] = right_product(jnp.concatenate(sums, axis=0), restrict_pair[...])

    def put(buffer, flat):
        for t in range(nt):
            for z in range(nz):
                s = t * nz + z
                buffer[t + 2, z + 2] = flat[s * cplane:(s + 1) * cplane]

    def shifted(buffer, dt, dz):
        return jnp.concatenate(
            [buffer[t + 2 + dt, z + 2 + dz] for t in range(nt) for z in range(nz)], axis=0
        )

    current = right_product(coarse_rhs[...], coarse_smooth[...])
    for sweep in range(SWEEPS):
        buffer = values.at[sweep]
        put(buffer, current)
        copies = send_z(buffer, 5 + sweep, 2) + send_t(buffer, 5 + sweep, 2)
        rest_copies += send_piece(1 + sweep)
        moved = dot(coarse_shuffle[...], stacked(current, 0))
        terms = [current] + [moved[k * crows:(k + 1) * crows] for k in range(4)]
        rest_coarse = coarse_rhs[...] - right_product(
            jnp.concatenate(terms, axis=1), coarse_near[...]
        )
        arrive(copies)
        terms = [shifted(buffer, dt, dz) for dt, dz in steps.values()]
        rest_coarse -= right_product(jnp.concatenate(terms, axis=1), coarse_hop[...])
        current += right_product(rest_coarse, coarse_smooth[...])
    buffer = values.at[SWEEPS]
    put(buffer, current)
    number = 5 + SWEEPS
    copies = send_z(buffer, number, 2, 2) + send_t(buffer, number, 2, 2)
    sides = [(t, z) for t in (0, 1) for z in (0, 1)]
    for index, (device, (t, z)) in enumerate(zip(diagonals, sides)):
        source = buffer.at[1 + nt if t else 2, 1 + nz if z else 2]
        target = buffer.at[1 if t else 2 + nt, 1 if z else 2 + nz]
        copies.append(send(number, 4 + index, source, target, device))

    def prolong(flat, places):
        lifted = stacked(left_product(prolong_pair[...], flat, NT), 1)
        wide = dot(lifted, spread[...])
        for s, (t, z) in enumerate(places):
            correction[t + 2, z + 2] = lanes(wide, s)

    prolong(current, [place for places in rows for place in places])
    local_terms(1, correction, r2, r3)
    arrive(copies)
    halo = [place for places in around for place in places]
    halo += [(t, z) for t in (-2, nt + 1) for z in range(nz)]
    halo += [(t, z) for t in range(nt) for z in (-2, nz + 1)]
    halo += [(t, z) for t in (-1, nt) for z in (-1, nz)]
    for begin in range(0, len(halo), sites):
        places = halo[begin:begin + sites]
        flat = [buffer[t + 2, z + 2] for t, z in places]
        flat += [jnp.zeros((cplane, cc), F32)] * (sites - len(places))
        prolong(jnp.concatenate(flat, axis=0), places)
    t_edges(1, correction, r3)
    z_edges(1, correction, r3)
    arrive(weight_copies)
    arrive(rest_copies)
    for places in around:
        all_terms(1, correction, r2, r3, places)

    for z in edges_first:
        all_terms(0, r3, r3, r4, columns[z])
        if z == 0:
            z_copies = send_low(r4, 3, 2)
        if z == nz - 1:
            z_copies += send_high(r4, 3, 2)
    t_copies = send_t(r4, 3, 2)
    local_terms(0, r4, r4, r5)
    for places in rows:
        wide = jnp.concatenate([
            r0[t + 2, z + 2] + r1[t + 2, z + 2] + r3[t + 2, z + 2] + r4[t + 2, z + 2]
            for t, z in places
        ], axis=1)
        wide = left_product(smooth_pair[...], wide)
        for s, (t, z) in enumerate(places):
            solution_ref[pl.ds(t * nz + z, cf, stride=sites), :] = (
                correction[t + 2, z + 2] + lanes(wide, s)
            )
    arrive(t_copies)
    t_edges(0, r4, r5)
    for places in columns[1:-1]:
        for t, z in places:
            residual_ref[pl.ds(t * nz + z, cf, stride=sites), :] = r5[t + 2, z + 2]
    arrive(z_copies)
    z_edges(0, r4, r5)
    for places in (columns[0], columns[-1]):
        for t, z in places:
            residual_ref[pl.ds(t * nz + z, cf, stride=sites), :] = r5[t + 2, z + 2]
    for copy in pending:
        copy.wait_send()


def solution(mesh):
    def shards(
        rhs_field, link_weights, fine_blocks, smoother, plane_next, aggregate,
        restrict_map, prolong_map, coarse_blocks, coarse_smoother, coarse_next,
    ):
        _, cf, nt, nz, plane = rhs_field.shape
        cplane = coarse_next.shape[1]
        cc = coarse_smoother.shape[0]
        sites = nt * nz
        crows = sites * cplane
        sizes = (
            nt, nz, cf, plane, cplane, cc,
            mesh.shape["col"], mesh.shape["ta"], mesh.shape["gz"],
        )
        out = jax.ShapeDtypeStruct((cf * sites, plane), F32)
        vmem = pl.BlockSpec(memory_space=pltpu.VMEM)
        hbm = pl.BlockSpec(memory_space=pltpu.HBM)
        operands = (
            rhs_field.reshape(cf * sites, plane), link_weights.reshape(-1, plane), fine_blocks,
            smoother, plane_next, aggregate.reshape(1, plane), restrict_map, prolong_map.T,
            coarse_blocks, coarse_smoother, coarse_next,
        )
        solved, residual = pl.pallas_call(
            functools.partial(kernel, sizes),
            out_shape=(out, out),
            in_specs=[hbm] * len(operands),
            out_specs=(vmem, vmem),
            scratch_shapes=[pltpu.VMEM(operand.shape, operand.dtype) for operand in operands] + [
                pltpu.VMEM((7, nt + 4, nz + 4, cf, plane), F32),
                pltpu.VMEM((1 + SWEEPS, nt + 4, nz + 4, cplane, cc), F32),
                pltpu.VMEM((nt + 2, nz + 2, 8, plane), F32),
                pltpu.VMEM((crows, cc), F32),
                pltpu.VMEM((2, 2 * cf, 9 * cf), BF16),
                pltpu.VMEM((2, 2 * cf, 8 * cf), BF16),
                pltpu.VMEM((2, 4, 2 * cf, cf), BF16),
                pltpu.VMEM((2 * cf, cf), BF16),
                pltpu.VMEM((2 * plane, 4 * plane), BF16),
                pltpu.VMEM((2 * crows, sites * plane), BF16),
                pltpu.VMEM((cf, 2 * cc), BF16),
                pltpu.VMEM((2 * cf, cc), BF16),
                pltpu.VMEM((5 * cc, 2 * cc), BF16),
                pltpu.VMEM((4 * cc, 2 * cc), BF16),
                pltpu.VMEM((cc, 2 * cc), BF16),
                pltpu.VMEM((4 * crows, 2 * crows), BF16),
                pltpu.SemaphoreType.DMA((len(operands),)),
                pltpu.SemaphoreType.DMA((7 + 2 * SWEEPS, 8)),
                pltpu.SemaphoreType.DMA((7 + 2 * SWEEPS, 8)),
            ],
            compiler_params=pltpu.CompilerParams(
                collective_id=0, has_side_effects=True, vmem_limit_bytes=63 * 1024 * 1024
            ),
        )(*operands)
        return solved.reshape(rhs_field.shape), residual.reshape(rhs_field.shape)

    return jax.shard_map(
        shards,
        mesh=mesh,
        in_specs=(
            P(None, None, ("ta", "col"), "gz", None),
            P(None, ("ta", "col"), "gz", None),
            P(), P(), P(), P(), P(), P(), P(), P(), P(),
        ),
        out_specs=(
            P(None, None, ("ta", "col"), "gz", None),
            P(None, None, ("ta", "col"), "gz", None),
        ),
        check_vma=False,
    )
```
